256 devices in a mesh: dp: 64 (over z, y_lo, x), lat: 4 (over y_hi, core).
Axes of the slice: x: 4, y: 4 (y_hi: 2, y_lo: 2; y = y_hi * 2 + y_lo), z: 8, core: 2. Of those that a mesh axis runs over, the one named last changes fastest.
Arguments:
- tokens: bfloat16 [196608, 512], P(('dp', 'lat')), may hold values from -6 to 6
- latents: bfloat16 [12288, 1024], P(('dp', 'lat')), may hold values from -6 to 6
- gain_self: float32 [512], replicated, may hold values from 0.1 to 1.9
- w_qkv_tok: bfloat16 [512, 1536], replicated, may hold values from -1 to 1
- w_o_tok: bfloat16 [512, 512], replicated, may hold values from -0.25 to 0.25
- gain_read: float32 [512], replicated, may hold values from 0.1 to 1.9
- w_kv_read: bfloat16 [512, 2048], replicated, may hold values from -1 to 1
- gain_lat: float32 [1024], replicated, may hold values from 0.1 to 1.9
- w_q_read: bfloat16 [1024, 1024], replicated, may hold values from -1 to 1
- gain_glob: float32 [1024], replicated, may hold values from 0.1 to 1.9
- w_qkv_glob: bfloat16 [3, 1024, 1024], P(None, None, 'lat'), may hold values from -1 to 1
- w_o_glob: bfloat16 [1024, 1024], P('lat'), may hold values from -0.375 to 0.375
- gain_write: float32 [512], replicated, may hold values from 0.1 to 1.9
- w_q_write: bfloat16 [512, 512], replicated, may hold values from -1 to 1
- gain_wlat: float32 [1024], replicated, may hold values from 0.1 to 1.9
- w_kv_write: bfloat16 [1024, 1024], replicated, may hold values from -1 to 1
Outputs:
- tokens_out: bfloat16 [196608, 512], P(('dp', 'lat'))
- latents_out: bfloat16 [12288, 1024], P(('dp', 'lat'))
The draws below stay inside these ranges and needn't reach their ends.
All inputs are finite; a program needn't handle non-finite values.
Results may differ from the reference program's by a relative error of at most 0.015.
Values may be sent and summed in bfloat16 or wider, within the bound.
No kernel may reach another device: no remote copies, remote signals or barrier semaphores. Data moves between devices by JAX's collectives and lax.ppermute only.
A program may use at most 128 MiB of HBM per device.

```python
import jax
import jax.numpy as jnp
from jax import lax

D = 512
DL = 1024
HEAD = 64
G = 256
NLAT = 16
TOKENS = 196608
LATENTS = 12288


image_count = 64


def spread_weight(key, salt, shape, fan_in):
    return jax.random.truncated_normal(jax.random.fold_in(key, salt), -6.0, 6.0, shape, jnp.float32) * fan_in ** (-0.5)


def activations(key, salt, rows, width):
    noise = jax.random.truncated_normal(jax.random.fold_in(key, salt), -6.0, 6.0, (rows, width), jnp.float32)
    return noise


def image_part(key, salt, rows, width):
    index = jnp.arange(rows, dtype=jnp.int32) * image_count // rows
    directions = jax.random.truncated_normal(jax.random.fold_in(key, salt), -4.0, 4.0, (image_count, width), jnp.float32)
    amplitude = jax.random.uniform(jax.random.fold_in(key, salt + 1), (image_count,), jnp.float32, 0.5, 1.0)
    return directions[index] * amplitude[index][:, None]


def draw_tokens(key, part):
    values = activations(key, 21, TOKENS, D)
    return values.astype(jnp.bfloat16)


def draw_latents(key, part):
    values = activations(key, 22, LATENTS, DL)
    values = values + image_part(key, 23, LATENTS, DL)
    values = jnp.clip(values, -6.0, 6.0)
    return values.astype(jnp.bfloat16)


def draw_w_qkv_tok(key, part):
    full = spread_weight(key, 31, (D, 3 * D), D)
    return full.astype(jnp.bfloat16)


def draw_w_q_read(key, part):
    full = spread_weight(key, 32, (DL, DL), DL)
    return full.astype(jnp.bfloat16)


def draw_w_kv_read(key, part):
    full = spread_weight(key, 33, (D, 2 * DL), D)
    return full.astype(jnp.bfloat16)


def draw_w_qkv_glob(key, part):
    factors = jnp.array([1.5, 1.5, 1.0], jnp.float32)
    full = spread_weight(key, 35, (3, DL, DL), DL) * factors[:, None, None]
    return full.astype(jnp.bfloat16)


def draw_w_q_write(key, part):
    full = spread_weight(key, 36, (D, D), D)
    return full.astype(jnp.bfloat16)


def draw_w_kv_write(key, part):
    full = spread_weight(key, 37, (DL, 2 * D), DL)
    return full.astype(jnp.bfloat16)


def steps_of(stream_key, shape, cuts, least, largest):
    factor_of = 1.0
    for position, parts in cuts:
        steps = jax.random.uniform(jax.random.fold_in(jax.random.fold_in(stream_key, 6), position), (parts,), jnp.float32, least / len(cuts), largest / len(cuts))
        factor_of = factor_of * jnp.repeat(jnp.exp(steps), shape[position] // parts).reshape((-1,) + (1,) * (len(shape) - 1 - position))
    return factor_of


def centred(key, extent, spread, reach, pieces=(), kind=jnp.bfloat16):
    entries = spread * jax.random.normal(key, extent, jnp.float32)
    if pieces:
        entries = entries * steps_of(key, extent, pieces, -0.22, 0.18)
    return jnp.clip(entries, -reach, reach).astype(kind)


def setup_inputs(seed: int = 0) -> dict:
    seeds = jax.random.split(jax.random.key(seed), 17)
    tokens = draw_tokens(jax.random.fold_in(seeds[16], 71), 0)
    latents = draw_latents(jax.random.fold_in(seeds[16], 71), 0)
    gain_self = jnp.clip(1.0 + 0.18 * jax.random.normal(seeds[2], (D,), jnp.float32), 0.1, 1.9)
    w_qkv_tok = draw_w_qkv_tok(jax.random.fold_in(seeds[16], 71), 0)
    w_o_tok = centred(seeds[4], (D, D), D ** -0.5, 0.25)
    gain_read = jnp.clip(1.0 + 0.18 * jax.random.normal(seeds[5], (D,), jnp.float32), 0.1, 1.9)
    w_kv_read = draw_w_kv_read(jax.random.fold_in(seeds[16], 71), 0)
    gain_lat = jnp.clip(1.0 + 0.18 * jax.random.normal(seeds[7], (DL,), jnp.float32), 0.1, 1.9)
    w_q_read = draw_w_q_read(jax.random.fold_in(seeds[16], 71), 0)
    gain_glob = jnp.clip(1.0 + 0.18 * jax.random.normal(seeds[9], (DL,), jnp.float32), 0.1, 1.9)
    w_qkv_glob = draw_w_qkv_glob(jax.random.fold_in(seeds[16], 71), 0)
    w_o_glob = centred(seeds[11], (DL, DL), (DL // 4) ** -0.5, 0.375, ((0, 4),))
    gain_write = jnp.clip(1.0 + 0.18 * jax.random.normal(seeds[12], (D,), jnp.float32), 0.1, 1.9)
    w_q_write = draw_w_q_write(jax.random.fold_in(seeds[16], 71), 0)
    gain_wlat = jnp.clip(1.0 + 0.18 * jax.random.normal(seeds[14], (DL,), jnp.float32), 0.1, 1.9)
    w_kv_write = draw_w_kv_write(jax.random.fold_in(seeds[16], 71), 0)
    return dict(tokens=tokens, latents=latents, gain_self=gain_self, w_qkv_tok=w_qkv_tok, w_o_tok=w_o_tok, gain_read=gain_read, w_kv_read=w_kv_read, gain_lat=gain_lat, w_q_read=w_q_read, gain_glob=gain_glob, w_qkv_glob=w_qkv_glob, w_o_glob=w_o_glob, gain_write=gain_write, w_q_write=w_q_write, gain_wlat=gain_wlat, w_kv_write=w_kv_write)


def rms_norm(values, gain):
    floats = values.astype(jnp.float32)
    factor = lax.rsqrt(lax.optimization_barrier(jnp.mean(floats * floats, axis=-1, keepdims=True)) + 1e-06)
    return (floats * factor * gain).astype(jnp.bfloat16)

def attend(query, keys, values):
    scores = jnp.einsum('qhe,khe->hqk', query.astype(jnp.float32), keys.astype(jnp.float32)) * HEAD ** (-0.5)
    peak = lax.optimization_barrier(jnp.max(scores, axis=-1, keepdims=True))
    weights = jnp.exp(scores - peak)
    total = lax.optimization_barrier(jnp.sum(weights, axis=-1))
    rounded = lax.optimization_barrier(weights.astype(jnp.bfloat16)).astype(jnp.float32)
    mixed = jnp.einsum('hqk,khe->hqe', rounded, values.astype(jnp.float32))
    return jnp.transpose(mixed / total[:, :, None], (1, 0, 2))

def front(inputs, gain_self, w_qkv_tok, w_o_tok, gain_read, w_kv_read, gain_lat, w_q_read):
    group, lat_rows = inputs
    rows = group.shape[0]
    packed = jnp.dot(rms_norm(group, gain_self), w_qkv_tok, preferred_element_type=jnp.float32)
    packed = packed.astype(jnp.bfloat16).reshape(rows, 3, -1, HEAD)
    mixed = attend(packed[:, 0], packed[:, 1], packed[:, 2]).reshape(rows, -1).astype(jnp.bfloat16)
    tokens_mid = (group.astype(jnp.float32) + jnp.dot(mixed, w_o_tok, preferred_element_type=jnp.float32)).astype(jnp.bfloat16)
    key_vals = jnp.dot(rms_norm(tokens_mid, gain_read), w_kv_read, preferred_element_type=jnp.float32)
    key_vals = key_vals.astype(jnp.bfloat16).reshape(rows, 2, -1, HEAD)
    query = jnp.dot(rms_norm(lat_rows, gain_lat), w_q_read, preferred_element_type=jnp.float32)
    query = query.astype(jnp.bfloat16).reshape(lat_rows.shape[0], -1, HEAD)
    read = attend(query, key_vals[:, 0], key_vals[:, 1]).reshape(lat_rows.shape[0], -1)
    return (tokens_mid, (lat_rows.astype(jnp.float32) + read).astype(jnp.bfloat16))

def back(inputs, gain_write, w_q_write, gain_wlat, w_kv_write):
    tokens_mid, lat_rows = inputs
    rows = tokens_mid.shape[0]
    query = jnp.dot(rms_norm(tokens_mid, gain_write), w_q_write, preferred_element_type=jnp.float32)
    query = query.astype(jnp.bfloat16).reshape(rows, -1, HEAD)
    key_vals = jnp.dot(rms_norm(lat_rows, gain_wlat), w_kv_write, preferred_element_type=jnp.float32)
    key_vals = key_vals.astype(jnp.bfloat16).reshape(lat_rows.shape[0], 2, -1, HEAD)
    written = attend(query, key_vals[:, 0], key_vals[:, 1]).reshape(rows, -1)
    return (tokens_mid.astype(jnp.float32) + written).astype(jnp.bfloat16)

def one_head(inputs):
    query, keys, values = inputs
    scores = jnp.dot(query, keys.T, preferred_element_type=jnp.float32) * HEAD ** (-0.5)
    peak = lax.optimization_barrier(jnp.max(scores, axis=-1, keepdims=True))
    weights = jnp.exp(scores - peak)
    total = lax.optimization_barrier(jnp.sum(weights, axis=-1, keepdims=True))
    mixed = jnp.dot(weights.astype(jnp.bfloat16), values, preferred_element_type=jnp.float32)
    return (mixed / total).astype(jnp.bfloat16)

def reference(tokens, latents, gain_self, w_qkv_tok, w_o_tok, gain_read, w_kv_read, gain_lat, w_q_read, gain_glob, w_qkv_glob, w_o_glob, gain_write, w_q_write, gain_wlat, w_kv_write):
    groups = tokens.reshape(-1, G, D)
    lat_groups = latents.reshape(-1, NLAT, DL)
    tokens_mid, latents_mid = lax.map(lambda pair: front(pair, gain_self, w_qkv_tok, w_o_tok, gain_read, w_kv_read, gain_lat, w_q_read), (groups, lat_groups))
    latents_mid = latents_mid.reshape(-1, DL)
    count = latents_mid.shape[0]
    normed = rms_norm(latents_mid, gain_glob)
    heads = []
    for which in range(3):
        projected = jnp.dot(normed, w_qkv_glob[which], preferred_element_type=jnp.float32).astype(jnp.bfloat16)
        heads.append(jnp.transpose(projected.reshape(count, -1, HEAD), (1, 0, 2)))
    mixed = lax.map(one_head, (heads[0], heads[1], heads[2]))
    mixed = jnp.transpose(mixed, (1, 0, 2)).reshape(count, -1)
    latents_out = (latents_mid.astype(jnp.float32) + jnp.dot(mixed, w_o_glob, preferred_element_type=jnp.float32)).astype(jnp.bfloat16)
    tokens_out = lax.map(lambda pair: back(pair, gain_write, w_q_write, gain_wlat, w_kv_write), (tokens_mid, latents_out.reshape(-1, NLAT, DL)))
    return (tokens_out.reshape(-1, D), latents_out)
```

```python
import functools

import jax
import jax.numpy as jnp
import numpy as np
from jax import lax
from jax.experimental import pallas as pl
from jax.experimental.pallas import tpu as pltpu
from jax.sharding import Mesh
from jax.sharding import PartitionSpec as P

HEAD = 64
G = 256
NLAT = 16
LOG2E = 1.4426950408889634
SCALE = LOG2E * HEAD ** (-0.5)

AXES = ("za", "zb", "zc", "yl", "x", "yh", "core")
SIZES = (2, 2, 2, 2, 4, 2, 2)
LAT = ("yh", "core")
HEADS4 = ("zc", "yl")
KEYS4 = ("za", "zb")
OUT64 = ("zc", "yl", "x", "yh", "core")

f32 = jnp.float32
bf16 = jnp.bfloat16


def dot(a, b):
    return jnp.dot(a, b, preferred_element_type=f32)


def dot_t(a, b):
    return lax.dot_general(a, b, (((1,), (1,)), ((), ())), preferred_element_type=f32)


def norm(values, gain):
    factor = lax.rsqrt(jnp.mean(values * values, axis=-1, keepdims=True) + 1e-06)
    return (values * factor * gain).astype(bf16)


def low_lanes(rows):
    return lax.broadcasted_iota(jnp.int32, (rows, 128), 1) < HEAD


def swap(values):
    return pltpu.roll(values, HEAD, 1)


def front_kernel(
    tok_ref, lat_ref, gself_ref, wqkv_ref, wo_ref, gread_ref, wkv_ref, glat_ref, wq_ref, gglob_ref,
    mid_ref, latmid_ref, normed_ref,
):
    x = tok_ref[...].astype(f32)
    packed = dot(norm(x, gself_ref[...]), wqkv_ref[...]).astype(bf16)
    low = low_lanes(G)
    zero = jnp.zeros((G, 128), bf16)
    one = jnp.ones((G, 128), bf16)
    pairs = []
    for p in range(4):
        q2 = packed[:, p * 128 : (p + 1) * 128]
        k2 = packed[:, 512 + p * 128 : 512 + (p + 1) * 128]
        v2 = packed[:, 1024 + p * 128 : 1024 + (p + 1) * 128]
        halves = []
        for half in range(2):
            here = low if half == 0 else jnp.logical_not(low)
            s = dot_t(jnp.where(here, q2, zero), k2) * SCALE
            w = jnp.exp2(s - jnp.max(s, axis=-1, keepdims=True))
            r = dot(w.astype(bf16), jnp.where(here, v2, one))
            halves.append(r / swap(r))
        pairs.append(jnp.where(low, halves[0], halves[1]).astype(bf16))
    mixed = jnp.concatenate(pairs, axis=1)
    mid = (x + dot(mixed, wo_ref[...])).astype(bf16)
    mid_ref[...] = mid
    kv = dot(norm(mid.astype(f32), gread_ref[...]), wkv_ref[...]).astype(bf16)
    lat = lat_ref[...].astype(f32)
    query = dot(norm(lat, glat_ref[...]), wq_ref[...]).astype(bf16)
    part = lax.broadcasted_iota(jnp.int32, (NLAT, 256), 1) // HEAD
    blocks = []
    for quad in range(4):
        q4 = query[:, quad * 256 : (quad + 1) * 256]
        k4 = kv[:, quad * 256 : (quad + 1) * 256]
        v4 = kv[:, 1024 + quad * 256 : 1024 + (quad + 1) * 256]
        stacked = jnp.concatenate(
            [jnp.where(part == a, q4, jnp.zeros_like(q4)) for a in range(4)], axis=0
        )
        s = dot_t(stacked, k4) * SCALE
        w = jnp.exp2(s - jnp.max(s, axis=-1, keepdims=True))
        r = dot(w.astype(bf16), v4) / jnp.sum(w, axis=-1, keepdims=True)
        got = jnp.zeros((NLAT, 256), f32)
        for a in range(4):
            got = jnp.where(part == a, r[a * NLAT : (a + 1) * NLAT], got)
        blocks.append(got)
    latmid = (lat + jnp.concatenate(blocks, axis=1)).astype(bf16)
    latmid_ref[...] = latmid
    normed_ref[...] = norm(latmid.astype(f32), gglob_ref[...])


def project_kernel(block_ref, w_ref, out_ref):
    block = block_ref[...]
    rows = block.shape[0]
    half = rows // 2
    q = dot(block, w_ref[0]).astype(bf16).astype(f32)
    k = dot(block, w_ref[1]).astype(bf16).astype(f32)
    v = dot(block, w_ref[2]).astype(bf16).astype(f32)
    low = low_lanes(rows)
    lowh = low_lanes(half)
    for pair in range(2):
        lanes = slice(pair * 128, (pair + 1) * 128)
        q2, k2, v2 = q[:, lanes], k[:, lanes], v[:, lanes]
        out_ref[2 * pair, :rows] = jnp.where(low, k2, swap(v2)).astype(bf16)
        out_ref[2 * pair + 1, :rows] = jnp.where(low, swap(k2), v2).astype(bf16)
        out_ref[2 * pair, rows:] = jnp.where(lowh, q2[:half], swap(q2[half:])).astype(bf16)
        out_ref[2 * pair + 1, rows:] = jnp.where(lowh, swap(q2[:half]), q2[half:]).astype(bf16)


def attend_kernel(
    place_ref, own_ref, kv1_ref, kv2_ref, kv3_ref, q1_ref, q2_ref, q3_ref, out_ref, keys, values
):
    rows = kv1_ref.shape[1]
    half = rows // 2
    low = low_lanes(rows)
    lowh = low_lanes(half)
    one = jnp.ones((rows, 128), bf16)
    for k, ref in enumerate((own_ref, kv1_ref, kv2_ref, kv3_ref)):
        for t in range(4):
            at = (k * 4 + t) * rows
            kv = ref[t, :rows]
            keys[at : at + rows, :] = kv
            values[at : at + rows, :] = jnp.where(low, one, kv)
    lane = lax.broadcasted_iota(jnp.int32, (rows, 128), 1)
    me = place_ref[0]
    for k, ref in enumerate((own_ref, q1_ref, q2_ref, q3_ref)):
        start = rows if k == 0 else 0

        def tile(t, carry, k=k, ref=ref, start=start):
            got = ref[t, start : start + half].astype(f32)
            zero = jnp.zeros_like(got)
            query = jnp.concatenate(
                [jnp.where(lowh, got, zero), jnp.where(lowh, swap(got), zero)], axis=0
            ).astype(bf16)
            s = dot_t(query, keys[...])
            peak = jnp.max(s, axis=-1, keepdims=True) * SCALE
            w = jnp.exp2(s * SCALE - peak)
            r = dot(w.astype(bf16), values[...])
            total = jnp.where(low, r, 1.0)
            size = peak + jnp.log2(total)
            hi = size.astype(bf16).astype(f32)
            mid = (size - hi).astype(bf16).astype(f32)
            low_part = size - hi - mid
            stats = jnp.where(lane == 0, hi, jnp.where(lane == 1, mid, low_part))
            out_ref[t, me ^ k] = jnp.where(low, stats, r / swap(r)).astype(bf16)
            return carry

        lax.fori_loop(0, 4, tile, 0)


def back_kernel(
    got_ref, latmid_ref, wo_ref, gwlat_ref, wkv_ref, mid_ref, gwrite_ref, wq_ref, tok_ref, lat_ref
):
    rows = latmid_ref.shape[0]
    low = low_lanes(rows)
    heads = [None] * 16
    for t in range(4):
        for lat in range(4):
            parts = [got_ref[t * 16 + x * 4 + lat].astype(f32) for x in range(4)]
            sizes = [
                jnp.sum(jnp.where(lax.broadcasted_iota(jnp.int32, (rows, 128), 1) < 3, p, 0.0), axis=-1, keepdims=True)
                for p in parts
            ]
            peak = functools.reduce(jnp.maximum, sizes)
            weights = [jnp.exp2(s - peak) for s in sizes]
            total = functools.reduce(lax.add, weights)
            mixed = functools.reduce(lax.add, [p * w for p, w in zip(parts, weights)])
            heads[lat * 4 + t] = mixed / total
    pairs = [jnp.where(low, swap(heads[2 * p]), heads[2 * p + 1]).astype(bf16) for p in range(8)]
    mixed = jnp.concatenate(pairs, axis=1)
    latents = (latmid_ref[...].astype(f32) + dot(mixed, wo_ref[...])).astype(bf16)
    lat_ref[...] = latents
    kv = dot(norm(latents.astype(f32), gwlat_ref[...]), wkv_ref[...]).astype(bf16)
    head_of_row = lax.broadcasted_iota(jnp.int32, (8 * NLAT, 512), 0) // NLAT
    head_of_lane = lax.broadcasted_iota(jnp.int32, (8 * NLAT, 512), 1) // HEAD
    here = head_of_row == head_of_lane
    ones = jnp.where(here, 1.0, 0.0).astype(bf16)
    for g in range(rows // NLAT):
        mid = mid_ref[g * G : (g + 1) * G, :].astype(f32)
        query = dot(norm(mid, gwrite_ref[...]), wq_ref[...]).astype(bf16)
        k = kv[g * NLAT : (g + 1) * NLAT, :512]
        v = kv[g * NLAT : (g + 1) * NLAT, 512:]
        zero = jnp.zeros((8 * NLAT, 512), bf16)
        k8 = jnp.where(here, jnp.concatenate([k] * 8, axis=0), zero)
        v8 = jnp.where(here, jnp.concatenate([v] * 8, axis=0), zero)
        s = (dot_t(k8, query) * SCALE).reshape(8, NLAT, G)
        w = jnp.exp2(s - jnp.max(s, axis=1, keepdims=True)).reshape(8 * NLAT, G).astype(bf16)
        turned = w.T
        written = dot(turned, v8) / dot(turned, ones)
        tok_ref[g * G : (g + 1) * G, :] = (mid + written).astype(bf16)


def params(megabytes):
    return pltpu.CompilerParams(vmem_limit_bytes=megabytes * 1024 * 1024)


def whole(array):
    return pl.BlockSpec(array.shape, lambda *_, n=len(array.shape): (0,) * n)


def local(
    tokens,
    latents,
    gain_self,
    w_qkv_tok,
    w_o_tok,
    gain_read,
    w_kv_read,
    gain_lat,
    w_q_read,
    gain_glob,
    w_qkv_glob,
    w_o_glob,
    gain_write,
    w_q_write,
    gain_wlat,
    w_kv_write,
):
    token_rows, width = tokens.shape
    lat_rows, lat_width = latents.shape
    groups = token_rows // G
    row = lambda gain: gain.reshape(1, -1)
    w_o_all = lax.all_gather(w_o_glob, LAT, axis=0, tiled=True)

    fixed = (
        row(gain_self), w_qkv_tok, w_o_tok, row(gain_read), w_kv_read, row(gain_lat), w_q_read,
        row(gain_glob),
    )
    tokens_mid, latents_mid, normed = pl.pallas_call(
        front_kernel,
        grid=(groups,),
        in_specs=[
            pl.BlockSpec((G, width), lambda g: (g, 0)),
            pl.BlockSpec((NLAT, lat_width), lambda g: (g, 0)),
        ]
        + [whole(a) for a in fixed],
        out_specs=[
            pl.BlockSpec((G, width), lambda g: (g, 0)),
            pl.BlockSpec((NLAT, lat_width), lambda g: (g, 0)),
            pl.BlockSpec((NLAT, lat_width), lambda g: (g, 0)),
        ],
        out_shape=[
            jax.ShapeDtypeStruct(tokens.shape, bf16),
            jax.ShapeDtypeStruct(latents.shape, bf16),
            jax.ShapeDtypeStruct(latents.shape, bf16),
        ],
        compiler_params=params(56),
        name="front",
    )(tokens, latents, *fixed)

    block = lax.all_gather(normed, LAT, axis=0, tiled=True)
    block_rows = block.shape[0]
    half = block_rows // 2
    sent = pl.pallas_call(
        project_kernel,
        out_shape=jax.ShapeDtypeStruct((4, block_rows + half, 128), bf16),
        compiler_params=params(56),
        name="project",
    )(block, w_qkv_glob)
    own = lax.all_to_all(sent, HEADS4, 0, 0, tiled=True)
    own_kv = own[:, :block_rows]
    own_q = own[:, block_rows:]
    others_q = [lax.ppermute(own_q, "x", [(i, i ^ k) for i in range(4)]) for k in (1, 2, 3)]
    others_kv = [lax.ppermute(own_kv, KEYS4, [(i, i ^ k) for i in range(4)]) for k in (1, 2, 3)]
    place = lax.axis_index("x").astype(jnp.int32).reshape(1)
    vmem = pl.BlockSpec(memory_space=pltpu.VMEM)
    partial = pl.pallas_call(
        attend_kernel,
        in_specs=[pl.BlockSpec(memory_space=pltpu.SMEM)] + [vmem] * 7,
        out_specs=vmem,
        out_shape=jax.ShapeDtypeStruct((4, 4, block_rows, 128), bf16),
        scratch_shapes=[
            pltpu.VMEM((16 * block_rows, 128), bf16),
            pltpu.VMEM((16 * block_rows, 128), bf16),
        ],
        compiler_params=params(56),
        name="attend",
    )(place, own, *others_kv, *others_q)
    got = lax.all_to_all(
        partial.reshape(64, lat_rows, 128), OUT64, 0, 0, tiled=True
    )
    tokens_out, latents_out = pl.pallas_call(
        back_kernel,
        out_shape=[
            jax.ShapeDtypeStruct(tokens.shape, bf16),
            jax.ShapeDtypeStruct(latents.shape, bf16),
        ],
        compiler_params=params(56),
        name="back",
    )(
        got, latents_mid, w_o_all, row(gain_wlat), w_kv_write, tokens_mid, row(gain_write), w_q_write
    )
    return (tokens_out, latents_out)


def solution(mesh):
    fine = Mesh(np.asarray(mesh.devices).reshape(SIZES), AXES)
    rows = P(AXES, None)
    placed = (
        rows,
        rows,
        P(),
        P(),
        P(),
        P(),
        P(),
        P(),
        P(),
        P(),
        P(None, None, LAT),
        P(LAT, None),
        P(),
        P(),
        P(),
        P(),
    )
    return jax.shard_map(
        local,
        mesh=fine,
        in_specs=placed,
        out_specs=(rows, rows),
        check_vma=False,
    )
```

```python
import functools

import jax
import jax.numpy as jnp
import numpy as np
from jax import lax
from jax.experimental import pallas as pl
from jax.experimental.pallas import tpu as pltpu
from jax.sharding import Mesh
from jax.sharding import PartitionSpec as P

HEAD = 64
G = 256
NLAT = 16
LOG2E = 1.4426950408889634
SCALE = LOG2E * HEAD ** (-0.5)

AXES = ("za", "zb", "zc", "yl", "x", "yh", "core")
SIZES = (2, 2, 2, 2, 4, 2, 2)
LAT = ("yh", "core")
HEADS4 = ("zc", "yl")
KEYS4 = ("za", "zb")
OUT64 = ("zc", "yl", "x", "yh", "core")

f32 = jnp.float32
bf16 = jnp.bfloat16


def dot(a, b):
    return jnp.dot(a, b, preferred_element_type=f32)


def dot_t(a, b):
    return lax.dot_general(a, b, (((1,), (1,)), ((), ())), preferred_element_type=f32)


def norm(values, gain):
    factor = lax.rsqrt(jnp.mean(values * values, axis=-1, keepdims=True) + 1e-06)
    return (values * factor * gain).astype(bf16)


def low_lanes(rows):
    return lax.broadcasted_iota(jnp.int32, (rows, 128), 1) < HEAD


def swap(values):
    return pltpu.roll(values, HEAD, 1)


def front_kernel(
    tok_ref, lat_ref, gself_ref, gread_ref, glat_ref, gglob_ref, wqkv_hbm, wo_hbm, wkv_hbm, wq_hbm,
    mid_ref, latmid_ref, normed_ref,
    wqkv, wo, wkv, wq, packed, kv, mixed, sems,
):
    copies = [
        pltpu.make_async_copy(source, target, sems.at[i])
        for i, (source, target) in enumerate(
            ((wqkv_hbm, wqkv), (wo_hbm, wo), (wq_hbm, wq), (wkv_hbm, wkv))
        )
    ]
    for copy in copies:
        copy.start()
    groups = tok_ref.shape[0] // G
    x = tok_ref[...].astype(f32)
    normed = norm(x, gself_ref[...])
    copies[0].wait()
    packed[...] = dot(normed, wqkv[...]).astype(bf16)
    low = low_lanes(G)
    zero = jnp.zeros((G, 128), bf16)
    for g in range(groups):
        rows = slice(g * G, (g + 1) * G)
        for p in range(4):
            q2 = packed[rows, p * 128 : (p + 1) * 128]
            k2 = packed[rows, 512 + p * 128 : 512 + (p + 1) * 128]
            v2 = packed[rows, 1024 + p * 128 : 1024 + (p + 1) * 128]
            both = jnp.concatenate([jnp.where(low, q2, zero), jnp.where(low, zero, q2)], axis=0)
            s = dot_t(both, k2) * SCALE
            w = jnp.exp2(s - jnp.max(s, axis=-1, keepdims=True))
            r = dot(w.astype(bf16), v2) / jnp.sum(w, axis=-1, keepdims=True)
            mixed[rows, p * 128 : (p + 1) * 128] = jnp.where(low, r[:G], r[G:]).astype(bf16)
    copies[1].wait()
    mid = (x + dot(mixed[...], wo[...])).astype(bf16)
    mid_ref[...] = mid
    normed = norm(mid.astype(f32), gread_ref[...])
    copies[2].wait()
    lat = lat_ref[...].astype(f32)
    query = dot(norm(lat, glat_ref[...]), wq[...]).astype(bf16)
    copies[3].wait()
    kv[...] = dot(normed, wkv[...]).astype(bf16)
    part = lax.broadcasted_iota(jnp.int32, (NLAT, 256), 1) // HEAD
    for g in range(groups):
        rows = slice(g * G, (g + 1) * G)
        mine = slice(g * NLAT, (g + 1) * NLAT)
        blocks = []
        for quad in range(4):
            q4 = query[mine, quad * 256 : (quad + 1) * 256]
            k4 = kv[rows, quad * 256 : (quad + 1) * 256]
            v4 = kv[rows, 1024 + quad * 256 : 1024 + (quad + 1) * 256]
            stacked = jnp.concatenate(
                [jnp.where(part == a, q4, jnp.zeros_like(q4)) for a in range(4)], axis=0
            )
            s = dot_t(stacked, k4) * SCALE
            w = jnp.exp2(s - jnp.max(s, axis=-1, keepdims=True))
            r = dot(w.astype(bf16), v4) / jnp.sum(w, axis=-1, keepdims=True)
            got = jnp.zeros((NLAT, 256), f32)
            for a in range(4):
                got = jnp.where(part == a, r[a * NLAT : (a + 1) * NLAT], got)
            blocks.append(got)
        latmid = (lat[mine] + jnp.concatenate(blocks, axis=1)).astype(bf16)
        latmid_ref[mine, :] = latmid
        normed_ref[mine, :] = norm(latmid.astype(f32), gglob_ref[...])


def project_kernel(block_ref, w_ref, out_ref):
    block = block_ref[...]
    rows = block.shape[0]
    half = rows // 2
    q = dot(block, w_ref[0]).astype(bf16).astype(f32)
    k = dot(block, w_ref[1]).astype(bf16).astype(f32)
    v = dot(block, w_ref[2]).astype(bf16).astype(f32)
    low = low_lanes(rows)
    lowh = low_lanes(half)
    for pair in range(2):
        lanes = slice(pair * 128, (pair + 1) * 128)
        q2, k2, v2 = q[:, lanes], k[:, lanes], v[:, lanes]
        out_ref[2 * pair, :rows] = jnp.where(low, k2, swap(v2)).astype(bf16)
        out_ref[2 * pair + 1, :rows] = jnp.where(low, swap(k2), v2).astype(bf16)
        out_ref[2 * pair, rows:] = jnp.where(lowh, q2[:half], swap(q2[half:])).astype(bf16)
        out_ref[2 * pair + 1, rows:] = jnp.where(lowh, swap(q2[:half]), q2[half:]).astype(bf16)


def unpack_queries(q_refs, starts, rows, queries):
    half = rows // 2
    low = low_lanes(half)
    for k, (ref, start) in enumerate(zip(q_refs, starts)):
        for t in range(4):
            got = ref[t, start : start + half].astype(f32)
            zero = jnp.zeros_like(got)
            at = (k * 4 + t) * rows
            both = jnp.concatenate(
                [jnp.where(low, got, zero), jnp.where(low, swap(got), zero)], axis=0
            )
            queries[at : at + rows, :] = both.astype(bf16)


def attend_part(queries, key_refs, rows, before, finish):
    keys = jnp.concatenate(
        [ref[t, :rows] for ref in key_refs for t in range(ref.shape[0])], axis=0
    )
    values = jnp.where(low_lanes(keys.shape[0]), jnp.ones_like(keys), keys)
    step = 4 * rows
    for k in range(4):
        at = slice(k * step, (k + 1) * step)
        s = dot_t(queries[at, :], keys) * SCALE
        peak = jnp.max(s, axis=-1, keepdims=True)
        if before is None:
            state = dot(jnp.exp2(s - peak).astype(bf16), values)
        else:
            old_peak = before[1, at, :]
            wide = jnp.maximum(peak, old_peak)
            peak = wide[:, :1]
            state = dot(jnp.exp2(s - peak).astype(bf16), values)
            state = state + before[0, at, :] * jnp.exp2(old_peak - wide)
        finish(k, state, peak)


def keep_state(state_ref, step):
    def keep(k, state, peak):
        state_ref[0, k * step : (k + 1) * step, :] = state
        state_ref[1, k * step : (k + 1) * step, :] = jnp.broadcast_to(peak, state.shape)

    return keep


def attend_first_kernel(own_ref, q1_ref, q2_ref, q3_ref, queries_ref, state_ref):
    rows = q1_ref.shape[1] * 2
    unpack_queries((own_ref, q1_ref, q2_ref, q3_ref), (rows, 0, 0, 0), rows, queries_ref)
    attend_part(queries_ref, (own_ref,), rows, None, keep_state(state_ref, 4 * rows))


def attend_next_kernel(queries_ref, kv1_ref, kv2_ref, before_ref, state_ref):
    rows = kv1_ref.shape[1]
    attend_part(
        queries_ref, (kv1_ref, kv2_ref), rows, before_ref, keep_state(state_ref, 4 * rows)
    )


def attend_last_kernel(place_ref, queries_ref, kv1_ref, kv2_ref, before_ref, out_ref):
    rows = kv1_ref.shape[1]
    unit = rows // 4
    half = unit // 2
    me = place_ref[0]
    low = low_lanes(half)
    lane = lax.broadcasted_iota(jnp.int32, (8, 128), 1)
    term = lax.rem(lane, 3)

    def send(k, state, peak):
        turned = swap(state)
        for t in range(4):
            for u in range(4):
                at = (t * 4 + u) * unit
                top = slice(at, at + half)
                end = slice(at + half, at + unit)
                packed = jnp.where(low, turned[top], state[end]) / jnp.where(
                    low, state[top], turned[end]
                )
                sums = jnp.ones((8, 128), f32)
                peaks = jnp.zeros((8, 128), f32)
                for a in range(unit // 8):
                    here = jnp.logical_and(lane >= 3 * a, lane < 3 * a + 3)
                    part = slice(at + 8 * a, at + 8 * a + 8)
                    sums = jnp.where(here, state[part], sums)
                    peaks = jnp.where(here, peak[part], peaks)
                size = peaks + jnp.log2(sums)
                first = size.astype(bf16).astype(f32)
                second = (size - first).astype(bf16).astype(f32)
                stats = jnp.where(
                    term == 0, first, jnp.where(term == 1, second, size - first - second)
                )
                out_ref[t, me ^ k, u * 32 : (u + 1) * 32] = jnp.concatenate(
                    [packed, stats], axis=0
                ).astype(bf16)

    attend_part(queries_ref, (kv1_ref, kv2_ref), rows, before_ref, send)


def write_query_kernel(mid_ref, gain_ref, w_ref, out_ref):
    out_ref[...] = dot(norm(mid_ref[...].astype(f32), gain_ref[...]), w_ref[...]).astype(bf16)


def back_kernel(
    got_ref, latmid_ref, gwlat_ref, mid_ref, query_ref, wo_hbm, wkv_hbm, tok_ref, lat_ref,
    wo, wkv, sems,
):
    copies = [
        pltpu.make_async_copy(source, target, sems.at[i])
        for i, (source, target) in enumerate(((wo_hbm, wo), (wkv_hbm, wkv)))
    ]
    for copy in copies:
        copy.start()
    rows = latmid_ref.shape[0]
    half = rows // 2
    low = low_lanes(half)
    low8 = low_lanes(8)
    heads = [None] * 16
    for t in range(4):
        for lat in range(4):
            parts = [got_ref[t * 16 + x * 4 + lat].astype(f32) for x in range(4)]
            sizes = [
                p[half:] + pltpu.roll(p[half:], 127, 1) + pltpu.roll(p[half:], 126, 1)
                for p in parts
            ]
            peak = functools.reduce(jnp.maximum, sizes)
            weights = [jnp.exp2(s - peak) for s in sizes]
            total = functools.reduce(lax.add, weights)
            mixed = jnp.zeros((half, 128), f32)
            for p, w in zip(parts, weights):
                share = w / total
                spread = [
                    jnp.where(low8, share[:, 3 * b : 3 * b + 1], share[:, c : c + 1])
                    for b, c in ((b, 3 * (b + half // 8)) for b in range(half // 8))
                ]
                mixed = mixed + p[:half] * jnp.concatenate(spread, axis=0)
            heads[lat * 4 + t] = mixed
    pairs = []
    for p in range(8):
        one, two = heads[2 * p], heads[2 * p + 1]
        top = jnp.where(low, one, swap(two))
        end = jnp.where(low, swap(one), two)
        pairs.append(jnp.concatenate([top, end], axis=0).astype(bf16))
    mixed = jnp.concatenate(pairs, axis=1)
    copies[0].wait()
    latents = (latmid_ref[...].astype(f32) + dot(mixed, wo[...])).astype(bf16)
    lat_ref[...] = latents
    normed = norm(latents.astype(f32), gwlat_ref[...])
    copies[1].wait()
    kv = dot(normed, wkv[...]).astype(bf16)
    head_of_row = lax.broadcasted_iota(jnp.int32, (8 * NLAT, 512), 0) // NLAT
    head_of_lane = lax.broadcasted_iota(jnp.int32, (8 * NLAT, 512), 1) // HEAD
    here = head_of_row == head_of_lane
    ones = jnp.where(here, 1.0, 0.0).astype(bf16)
    for g in range(rows // NLAT):
        mid = mid_ref[g * G : (g + 1) * G, :].astype(f32)
        query = query_ref[g * G : (g + 1) * G, :]
        k = kv[g * NLAT : (g + 1) * NLAT, :512]
        v = kv[g * NLAT : (g + 1) * NLAT, 512:]
        zero = jnp.zeros((8 * NLAT, 512), bf16)
        k8 = jnp.where(here, jnp.concatenate([k] * 8, axis=0), zero)
        v8 = jnp.where(here, jnp.concatenate([v] * 8, axis=0), zero)
        s = (dot_t(k8, query) * SCALE).reshape(8, NLAT, G)
        w = jnp.exp2(s - jnp.max(s, axis=1, keepdims=True)).reshape(8 * NLAT, G).astype(bf16)
        turned = w.T
        written = dot(turned, v8) / dot(turned, ones)
        tok_ref[g * G : (g + 1) * G, :] = (mid + written).astype(bf16)


def params(megabytes):
    return pltpu.CompilerParams(vmem_limit_bytes=megabytes * 1024 * 1024)


def cost(flops, bytes_accessed, transcendentals=0):
    return pl.CostEstimate(
        flops=int(flops), bytes_accessed=int(bytes_accessed), transcendentals=int(transcendentals)
    )


def local(
    tokens,
    latents,
    gain_self,
    w_qkv_tok,
    w_o_tok,
    gain_read,
    w_kv_read,
    gain_lat,
    w_q_read,
    gain_glob,
    w_qkv_glob,
    w_o_glob,
    gain_write,
    w_q_write,
    gain_wlat,
    w_kv_write,
):
    token_rows, width = tokens.shape
    lat_rows, lat_width = latents.shape
    row = lambda gain: gain.reshape(1, -1)
    vmem = pl.BlockSpec(memory_space=pltpu.VMEM)
    hbm = pl.BlockSpec(memory_space=pl.ANY)
    weights = (w_qkv_tok, w_o_tok, w_kv_read, w_q_read)
    tokens_mid, latents_mid, normed = pl.pallas_call(
        front_kernel,
        in_specs=[vmem] * 6 + [hbm] * 4,
        out_specs=[vmem] * 3,
        out_shape=[
            jax.ShapeDtypeStruct(tokens.shape, bf16),
            jax.ShapeDtypeStruct(latents.shape, bf16),
            jax.ShapeDtypeStruct(latents.shape, bf16),
        ],
        scratch_shapes=[pltpu.VMEM(w.shape, bf16) for w in weights]
        + [
            pltpu.VMEM((token_rows, w_qkv_tok.shape[1]), bf16),
            pltpu.VMEM((token_rows, w_kv_read.shape[1]), bf16),
            pltpu.VMEM((token_rows, width), bf16),
            pltpu.SemaphoreType.DMA((4,)),
        ],
        compiler_params=params(60),
        name="front",
    )(
        tokens, latents, row(gain_self), row(gain_read), row(gain_lat), row(gain_glob), *weights
    )

    block = lax.all_gather(normed, LAT, axis=0, tiled=True)
    block_rows = block.shape[0]
    half = block_rows // 2
    sent = pl.pallas_call(
        project_kernel,
        in_specs=[vmem] * 2,
        out_specs=vmem,
        out_shape=jax.ShapeDtypeStruct((4, block_rows + half, 128), bf16),
        compiler_params=params(32),
        name="project",
    )(block, w_qkv_glob)
    own = lax.all_to_all(sent, HEADS4, 0, 0, tiled=True)
    own, w_o_here = lax.optimization_barrier((own, w_o_glob))
    w_o_all = lax.all_gather(w_o_here, LAT, axis=0, tiled=True)
    own_kv = own[:, :block_rows]
    own_q = own[:, block_rows:]
    others_q = [lax.ppermute(own_q, "x", [(i, i ^ k) for i in range(4)]) for k in (1, 2, 3)]
    ahead = [(i, (i + 1) % 4) for i in range(4)]
    behind = [(i, (i - 1) % 4) for i in range(4)]
    kv_ahead = lax.ppermute(own_kv, KEYS4, ahead)
    kv_behind = lax.ppermute(own_kv, KEYS4, behind)
    kv_far1 = lax.ppermute(kv_ahead[:2], KEYS4, ahead)
    kv_far2 = lax.ppermute(kv_behind[2:], KEYS4, behind)
    place = lax.axis_index("x").astype(jnp.int32).reshape(1)
    many = 16 * block_rows

    def part_cost(parts):
        return cost(parts * many * many * 64, many * 128 * 10, parts * many * many // 4)

    queries, state = pl.pallas_call(
        attend_first_kernel,
        in_specs=[vmem] * 4,
        out_specs=[vmem] * 2,
        out_shape=[
            jax.ShapeDtypeStruct((many, 128), bf16),
            jax.ShapeDtypeStruct((2, many, 128), f32),
        ],
        compiler_params=params(32),
        cost_estimate=part_cost(1),
        name="attend_first",
    )(own, *others_q)
    state = pl.pallas_call(
        attend_next_kernel,
        in_specs=[vmem] * 4,
        out_specs=vmem,
        out_shape=jax.ShapeDtypeStruct((2, many, 128), f32),
        compiler_params=params(32),
        cost_estimate=part_cost(2),
        name="attend_next",
    )(queries, kv_ahead, kv_behind, state)
    message = 2 * lat_rows // 3
    partial = pl.pallas_call(
        attend_last_kernel,
        in_specs=[pl.BlockSpec(memory_space=pltpu.SMEM)] + [vmem] * 4,
        out_specs=vmem,
        out_shape=jax.ShapeDtypeStruct((4, 4, 4 * message, 128), bf16),
        compiler_params=params(32),
        cost_estimate=part_cost(1),
        name="attend_last",
    )(place, queries, kv_far1, kv_far2, state)
    got = lax.all_to_all(partial.reshape(64, message, 128), OUT64, 0, 0, tiled=True)
    tokens_late, partial = lax.optimization_barrier((tokens_mid, partial))
    query = pl.pallas_call(
        write_query_kernel,
        in_specs=[vmem] * 3,
        out_specs=vmem,
        out_shape=jax.ShapeDtypeStruct(tokens.shape, bf16),
        compiler_params=params(32),
        cost_estimate=cost(2 * token_rows * width * width, token_rows * width * 4),
        name="write_query",
    )(tokens_late, row(gain_write), w_q_write)
    tokens_out, latents_out = pl.pallas_call(
        back_kernel,
        in_specs=[vmem] * 5 + [hbm] * 2,
        out_specs=[vmem] * 2,
        out_shape=[
            jax.ShapeDtypeStruct(tokens.shape, bf16),
            jax.ShapeDtypeStruct(latents.shape, bf16),
        ],
        scratch_shapes=[
            pltpu.VMEM(w_o_all.shape, bf16),
            pltpu.VMEM(w_kv_write.shape, bf16),
            pltpu.SemaphoreType.DMA((2,)),
        ],
        compiler_params=params(51),
        name="back",
    )(got, latents_mid, row(gain_wlat), tokens_late, query, w_o_all, w_kv_write)
    return (tokens_out, latents_out)


def solution(mesh):
    fine = Mesh(np.asarray(mesh.devices).reshape(SIZES), AXES)
    rows = P(AXES, None)
    placed = (
        rows,
        rows,
        P(),
        P(),
        P(),
        P(),
        P(),
        P(),
        P(),
        P(),
        P(None, None, LAT),
        P(LAT, None),
        P(),
        P(),
        P(),
        P(),
    )
    return jax.shard_map(
        local,
        mesh=fine,
        in_specs=placed,
        out_specs=(rows, rows),
        check_vma=False,
    )
```

```python
import functools

import jax
import jax.numpy as jnp
import numpy as np
from jax import lax
from jax.experimental import pallas as pl
from jax.experimental.pallas import tpu as pltpu
from jax.sharding import Mesh
from jax.sharding import PartitionSpec as P

HEAD = 64
G = 256
NLAT = 16
LOG2E = 1.4426950408889634
SCALE = LOG2E * HEAD ** (-0.5)

AXES = ("za", "zb", "zc", "yl", "x", "yh", "core")
SIZES = (2, 2, 2, 2, 4, 2, 2)
LAT = ("yh", "core")
HEADS4 = ("zc", "yl")
KEYS4 = ("za", "zb")
OUT64 = ("zc", "yl", "x", "yh", "core")

f32 = jnp.float32
bf16 = jnp.bfloat16


def dot(a, b):
    return jnp.dot(a, b, preferred_element_type=f32)


def dot_t(a, b):
    return lax.dot_general(a, b, (((1,), (1,)), ((), ())), preferred_element_type=f32)


def norm(values, gain):
    factor = lax.rsqrt(jnp.mean(values * values, axis=-1, keepdims=True) + 1e-06)
    return (values * factor * gain).astype(bf16)


def low_lanes(rows):
    return lax.broadcasted_iota(jnp.int32, (rows, 128), 1) < HEAD


def swap(values):
    return pltpu.roll(values, HEAD, 1)


def front_kernel(
    tok_ref, lat_ref, gself_ref, gread_ref, glat_ref, gglob_ref, wqkv_hbm, wo_hbm, wkv_hbm, wq_hbm,
    mid_ref, latmid_ref, normed_ref,
    wqkv, wo, wkv, wq, packed, kv, mixed, sems,
):
    copies = [
        pltpu.make_async_copy(source, target, sems.at[i])
        for i, (source, target) in enumerate(
            ((wqkv_hbm, wqkv), (wo_hbm, wo), (wq_hbm, wq), (wkv_hbm, wkv))
        )
    ]
    for copy in copies:
        copy.start()
    groups = tok_ref.shape[0] // G
    x = tok_ref[...].astype(f32)
    normed = norm(x, gself_ref[...])
    copies[0].wait()
    packed[...] = dot(normed, wqkv[...]).astype(bf16)
    low = low_lanes(G)
    zero = jnp.zeros((G, 128), bf16)
    for g in range(groups):
        rows = slice(g * G, (g + 1) * G)
        for p in range(4):
            q2 = packed[rows, p * 128 : (p + 1) * 128]
            k2 = packed[rows, 512 + p * 128 : 512 + (p + 1) * 128]
            v2 = packed[rows, 1024 + p * 128 : 1024 + (p + 1) * 128]
            both = jnp.concatenate([jnp.where(low, q2, zero), jnp.where(low, zero, q2)], axis=0)
            s = dot_t(both, k2) * SCALE
            w = jnp.exp2(s - jnp.max(s, axis=-1, keepdims=True))
            r = dot(w.astype(bf16), v2) / jnp.sum(w, axis=-1, keepdims=True)
            mixed[rows, p * 128 : (p + 1) * 128] = jnp.where(low, r[:G], r[G:]).astype(bf16)
    copies[1].wait()
    mid = (x + dot(mixed[...], wo[...])).astype(bf16)
    mid_ref[...] = mid
    normed = norm(mid.astype(f32), gread_ref[...])
    copies[2].wait()
    lat = lat_ref[...].astype(f32)
    query = dot(norm(lat, glat_ref[...]), wq[...]).astype(bf16)
    copies[3].wait()
    kv[...] = dot(normed, wkv[...]).astype(bf16)
    part = lax.broadcasted_iota(jnp.int32, (NLAT, 256), 1) // HEAD
    for g in range(groups):
        rows = slice(g * G, (g + 1) * G)
        mine = slice(g * NLAT, (g + 1) * NLAT)
        blocks = []
        for quad in range(4):
            q4 = query[mine, quad * 256 : (quad + 1) * 256]
            k4 = kv[rows, quad * 256 : (quad + 1) * 256]
            v4 = kv[rows, 1024 + quad * 256 : 1024 + (quad + 1) * 256]
            stacked = jnp.concatenate(
                [jnp.where(part == a, q4, jnp.zeros_like(q4)) for a in range(4)], axis=0
            )
            s = dot_t(stacked, k4) * SCALE
            w = jnp.exp2(s - jnp.max(s, axis=-1, keepdims=True))
            r = dot(w.astype(bf16), v4) / jnp.sum(w, axis=-1, keepdims=True)
            got = jnp.zeros((NLAT, 256), f32)
            for a in range(4):
                got = jnp.where(part == a, r[a * NLAT : (a + 1) * NLAT], got)
            blocks.append(got)
        latmid = (lat[mine] + jnp.concatenate(blocks, axis=1)).astype(bf16)
        latmid_ref[mine, :] = latmid
        normed_ref[mine, :] = norm(latmid.astype(f32), gglob_ref[...])


def project_kernel(block_ref, w_ref, out_ref):
    block = block_ref[...]
    rows = block.shape[0]
    half = rows // 2
    q = dot(block, w_ref[0]).astype(bf16).astype(f32)
    k = dot(block, w_ref[1]).astype(bf16).astype(f32)
    v = dot(block, w_ref[2]).astype(bf16).astype(f32)
    low = low_lanes(rows)
    lowh = low_lanes(half)
    for pair in range(2):
        lanes = slice(pair * 128, (pair + 1) * 128)
        q2, k2, v2 = q[:, lanes], k[:, lanes], v[:, lanes]
        out_ref[2 * pair, :rows] = jnp.where(low, k2, swap(v2)).astype(bf16)
        out_ref[2 * pair + 1, :rows] = jnp.where(low, swap(k2), v2).astype(bf16)
        out_ref[2 * pair, rows:] = jnp.where(lowh, q2[:half], swap(q2[half:])).astype(bf16)
        out_ref[2 * pair + 1, rows:] = jnp.where(lowh, swap(q2[:half]), q2[half:]).astype(bf16)


def unpack_queries(q_refs, starts, rows, queries):
    half = rows // 2
    low = low_lanes(half)
    for k, (ref, start) in enumerate(zip(q_refs, starts)):
        for t in range(4):
            got = ref[t, start : start + half].astype(f32)
            zero = jnp.zeros_like(got)
            at = (k * 4 + t) * rows
            both = jnp.concatenate(
                [jnp.where(low, got, zero), jnp.where(low, swap(got), zero)], axis=0
            )
            queries[at : at + rows, :] = both.astype(bf16)


def attend_part(queries, key_refs, rows, before, finish):
    keys = jnp.concatenate(
        [ref[t, :rows] for ref in key_refs for t in range(ref.shape[0])], axis=0
    )
    values = jnp.where(low_lanes(keys.shape[0]), jnp.ones_like(keys), keys)
    step = 4 * rows
    for k in range(4):
        at = slice(k * step, (k + 1) * step)
        s = dot_t(queries[at, :], keys) * SCALE
        peak = jnp.max(s, axis=-1, keepdims=True)
        if before is None:
            state = dot(jnp.exp2(s - peak).astype(bf16), values)
        else:
            old_peak = before[1, at, :]
            wide = jnp.maximum(peak, old_peak)
            peak = wide[:, :1]
            state = dot(jnp.exp2(s - peak).astype(bf16), values)
            state = state + before[0, at, :] * jnp.exp2(old_peak - wide)
        finish(k, state, peak)


def keep_state(state_ref, step):
    def keep(k, state, peak):
        state_ref[0, k * step : (k + 1) * step, :] = state
        state_ref[1, k * step : (k + 1) * step, :] = jnp.broadcast_to(peak, state.shape)

    return keep


def attend_first_kernel(own_ref, q1_ref, q2_ref, q3_ref, queries_ref, state_ref):
    rows = q1_ref.shape[1] * 2
    unpack_queries((own_ref, q1_ref, q2_ref, q3_ref), (rows, 0, 0, 0), rows, queries_ref)
    attend_part(queries_ref, (own_ref,), rows, None, keep_state(state_ref, 4 * rows))


def attend_next_kernel(queries_ref, kv1_ref, kv2_ref, before_ref, state_ref):
    rows = kv1_ref.shape[1]
    attend_part(
        queries_ref, (kv1_ref, kv2_ref), rows, before_ref, keep_state(state_ref, 4 * rows)
    )


def attend_last_kernel(place_ref, queries_ref, kv1_ref, kv2_ref, before_ref, out_ref):
    rows = kv1_ref.shape[1]
    unit = rows // 4
    half = unit // 2
    me = place_ref[0]
    low = low_lanes(half)
    lane = lax.broadcasted_iota(jnp.int32, (8, 128), 1)
    term = lax.rem(lane, 3)

    def send(k, state, peak):
        turned = swap(state)
        for t in range(4):
            for u in range(4):
                at = (t * 4 + u) * unit
                top = slice(at, at + half)
                end = slice(at + half, at + unit)
                packed = jnp.where(low, turned[top], state[end]) / jnp.where(
                    low, state[top], turned[end]
                )
                sums = jnp.ones((8, 128), f32)
                peaks = jnp.zeros((8, 128), f32)
                for a in range(unit // 8):
                    here = jnp.logical_and(lane >= 3 * a, lane < 3 * a + 3)
                    part = slice(at + 8 * a, at + 8 * a + 8)
                    sums = jnp.where(here, state[part], sums)
                    peaks = jnp.where(here, peak[part], peaks)
                size = peaks + jnp.log2(sums)
                first = size.astype(bf16).astype(f32)
                second = (size - first).astype(bf16).astype(f32)
                stats = jnp.where(
                    term == 0, first, jnp.where(term == 1, second, size - first - second)
                )
                out_ref[t, me ^ k, u * 32 : (u + 1) * 32] = jnp.concatenate(
                    [packed, stats], axis=0
                ).astype(bf16)

    attend_part(queries_ref, (kv1_ref, kv2_ref), rows, before_ref, send)


def write_query_kernel(mid_ref, gain_ref, w_ref, out_ref):
    out_ref[...] = dot(norm(mid_ref[...].astype(f32), gain_ref[...]), w_ref[...]).astype(bf16)


def back_kernel(
    place_ref, got_ref, latmid_ref, gwlat_ref, mid_ref, query_ref, wo0, wo1, wo2, wo3, wkv_hbm,
    tok_ref, lat_ref,
    wo, wkv, sems,
):
    moves = [(source, wo.at[i]) for i, source in enumerate((wo0, wo1, wo2, wo3))]
    copies = [
        pltpu.make_async_copy(source, target, sems.at[i])
        for i, (source, target) in enumerate(moves + [(wkv_hbm, wkv)])
    ]
    for copy in copies:
        copy.start()
    me = place_ref[0]
    rows = latmid_ref.shape[0]
    half = rows // 2
    low = low_lanes(half)
    low8 = low_lanes(8)
    latents = latmid_ref[...].astype(f32)
    for d in range(4):
        heads = []
        for t in range(4):
            parts = [got_ref[t * 16 + x * 4 + (me ^ d)].astype(f32) for x in range(4)]
            sizes = [
                p[half:] + pltpu.roll(p[half:], 127, 1) + pltpu.roll(p[half:], 126, 1)
                for p in parts
            ]
            peak = functools.reduce(jnp.maximum, sizes)
            weights = [jnp.exp2(s - peak) for s in sizes]
            total = functools.reduce(lax.add, weights)
            mixed = jnp.zeros((half, 128), f32)
            for p, w in zip(parts, weights):
                share = w / total
                spread = [
                    jnp.where(low8, share[:, 3 * b : 3 * b + 1], share[:, c : c + 1])
                    for b, c in ((b, 3 * (b + half // 8)) for b in range(half // 8))
                ]
                mixed = mixed + p[:half] * jnp.concatenate(spread, axis=0)
            heads.append(mixed)
        pairs = []
        for one, two in ((heads[0], heads[1]), (heads[2], heads[3])):
            top = jnp.where(low, one, swap(two))
            end = jnp.where(low, swap(one), two)
            pairs.append(jnp.concatenate([top, end], axis=0).astype(bf16))
        copies[d].wait()
        latents = latents + dot(jnp.concatenate(pairs, axis=1), wo[d])
    latents = latents.astype(bf16)
    lat_ref[...] = latents
    normed = norm(latents.astype(f32), gwlat_ref[...])
    copies[4].wait()
    kv = dot(normed, wkv[...]).astype(bf16)
    head_of_row = lax.broadcasted_iota(jnp.int32, (8 * NLAT, 512), 0) // NLAT
    head_of_lane = lax.broadcasted_iota(jnp.int32, (8 * NLAT, 512), 1) // HEAD
    here = head_of_row == head_of_lane
    ones = jnp.where(here, 1.0, 0.0).astype(bf16)
    for g in range(rows // NLAT):
        mid = mid_ref[g * G : (g + 1) * G, :].astype(f32)
        query = query_ref[g * G : (g + 1) * G, :]
        k = kv[g * NLAT : (g + 1) * NLAT, :512]
        v = kv[g * NLAT : (g + 1) * NLAT, 512:]
        zero = jnp.zeros((8 * NLAT, 512), bf16)
        k8 = jnp.where(here, jnp.concatenate([k] * 8, axis=0), zero)
        v8 = jnp.where(here, jnp.concatenate([v] * 8, axis=0), zero)
        s = (dot_t(k8, query) * SCALE).reshape(8, NLAT, G)
        w = jnp.exp2(s - jnp.max(s, axis=1, keepdims=True)).reshape(8 * NLAT, G).astype(bf16)
        turned = w.T
        written = dot(turned, v8) / dot(turned, ones)
        tok_ref[g * G : (g + 1) * G, :] = (mid + written).astype(bf16)


def params(megabytes):
    return pltpu.CompilerParams(vmem_limit_bytes=megabytes * 1024 * 1024)


def cost(flops, bytes_accessed, transcendentals=0):
    return pl.CostEstimate(
        flops=int(flops), bytes_accessed=int(bytes_accessed), transcendentals=int(transcendentals)
    )


def local(
    tokens,
    latents,
    gain_self,
    w_qkv_tok,
    w_o_tok,
    gain_read,
    w_kv_read,
    gain_lat,
    w_q_read,
    gain_glob,
    w_qkv_glob,
    w_o_glob,
    gain_write,
    w_q_write,
    gain_wlat,
    w_kv_write,
):
    token_rows, width = tokens.shape
    lat_rows, lat_width = latents.shape
    row = lambda gain: gain.reshape(1, -1)
    other = [(0, 1), (1, 0)]
    w_o_core = lax.ppermute(w_o_glob, "core", other)
    w_o_yh = lax.ppermute(w_o_glob, "yh", other)
    vmem = pl.BlockSpec(memory_space=pltpu.VMEM)
    hbm = pl.BlockSpec(memory_space=pl.ANY)
    weights = (w_qkv_tok, w_o_tok, w_kv_read, w_q_read)
    tokens_mid, latents_mid, normed = pl.pallas_call(
        front_kernel,
        in_specs=[vmem] * 6 + [hbm] * 4,
        out_specs=[vmem] * 3,
        out_shape=[
            jax.ShapeDtypeStruct(tokens.shape, bf16),
            jax.ShapeDtypeStruct(latents.shape, bf16),
            jax.ShapeDtypeStruct(latents.shape, bf16),
        ],
        scratch_shapes=[pltpu.VMEM(w.shape, bf16) for w in weights]
        + [
            pltpu.VMEM((token_rows, w_qkv_tok.shape[1]), bf16),
            pltpu.VMEM((token_rows, w_kv_read.shape[1]), bf16),
            pltpu.VMEM((token_rows, width), bf16),
            pltpu.SemaphoreType.DMA((4,)),
        ],
        compiler_params=params(60),
        name="front",
    )(
        tokens, latents, row(gain_self), row(gain_read), row(gain_lat), row(gain_glob), *weights
    )

    block = lax.all_gather(normed, LAT, axis=0, tiled=True)
    block_rows = block.shape[0]
    half = block_rows // 2
    sent = pl.pallas_call(
        project_kernel,
        in_specs=[vmem] * 2,
        out_specs=vmem,
        out_shape=jax.ShapeDtypeStruct((4, block_rows + half, 128), bf16),
        compiler_params=params(32),
        name="project",
    )(block, w_qkv_glob)
    own = lax.all_to_all(sent, HEADS4, 0, 0, tiled=True)
    own_kv = own[:, :block_rows]
    own_q = own[:, block_rows:]
    others_q = [lax.ppermute(own_q, "x", [(i, i ^ k) for i in range(4)]) for k in (1, 2, 3)]
    ahead = [(i, (i + 1) % 4) for i in range(4)]
    behind = [(i, (i - 1) % 4) for i in range(4)]
    kv_ahead = lax.ppermute(own_kv, KEYS4, ahead)
    kv_behind = lax.ppermute(own_kv, KEYS4, behind)
    kv_far1 = lax.ppermute(kv_ahead[:2], KEYS4, ahead)
    kv_far2 = lax.ppermute(kv_behind[2:], KEYS4, behind)
    place = lax.axis_index("x").astype(jnp.int32).reshape(1)
    many = 16 * block_rows

    def part_cost(parts):
        return cost(parts * many * many * 64, many * 128 * 10, parts * many * many // 4)

    queries, state = pl.pallas_call(
        attend_first_kernel,
        in_specs=[vmem] * 4,
        out_specs=[vmem] * 2,
        out_shape=[
            jax.ShapeDtypeStruct((many, 128), bf16),
            jax.ShapeDtypeStruct((2, many, 128), f32),
        ],
        compiler_params=params(32),
        cost_estimate=part_cost(1),
        name="attend_first",
    )(own, *others_q)
    state = pl.pallas_call(
        attend_next_kernel,
        in_specs=[vmem] * 4,
        out_specs=vmem,
        out_shape=jax.ShapeDtypeStruct((2, many, 128), f32),
        compiler_params=params(32),
        cost_estimate=part_cost(2),
        name="attend_next",
    )(queries, kv_ahead, kv_behind, state)
    message = 2 * lat_rows // 3
    partial = pl.pallas_call(
        attend_last_kernel,
        in_specs=[pl.BlockSpec(memory_space=pltpu.SMEM)] + [vmem] * 4,
        out_specs=vmem,
        out_shape=jax.ShapeDtypeStruct((4, 4, 4 * message, 128), bf16),
        compiler_params=params(32),
        cost_estimate=part_cost(1),
        name="attend_last",
    )(place, queries, kv_far1, kv_far2, state)
    got = lax.all_to_all(partial.reshape(64, message, 128), OUT64, 0, 0, tiled=True)
    tokens_late, w_o_late, partial = lax.optimization_barrier((tokens_mid, w_o_yh, partial))
    w_o_both = lax.ppermute(w_o_late, "core", other)
    query = pl.pallas_call(
        write_query_kernel,
        in_specs=[vmem] * 3,
        out_specs=vmem,
        out_shape=jax.ShapeDtypeStruct(tokens.shape, bf16),
        compiler_params=params(32),
        cost_estimate=cost(2 * token_rows * width * width, token_rows * width * 4),
        name="write_query",
    )(tokens_late, row(gain_write), w_q_write)
    tokens_out, latents_out = pl.pallas_call(
        back_kernel,
        in_specs=[pl.BlockSpec(memory_space=pltpu.SMEM)] + [vmem] * 5 + [hbm] * 5,
        out_specs=[vmem] * 2,
        out_shape=[
            jax.ShapeDtypeStruct(tokens.shape, bf16),
            jax.ShapeDtypeStruct(latents.shape, bf16),
        ],
        scratch_shapes=[
            pltpu.VMEM((4,) + w_o_glob.shape, bf16),
            pltpu.VMEM(w_kv_write.shape, bf16),
            pltpu.SemaphoreType.DMA((5,)),
        ],
        compiler_params=params(49),
        name="back",
    )(
        lax.axis_index(LAT).astype(jnp.int32).reshape(1),
        got,
        latents_mid,
        row(gain_wlat),
        tokens_late,
        query,
        w_o_glob,
        w_o_core,
        w_o_late,
        w_o_both,
        w_kv_write,
    )
    return (tokens_out, latents_out)


def solution(mesh):
    fine = Mesh(np.asarray(mesh.devices).reshape(SIZES), AXES)
    rows = P(AXES, None)
    placed = (
        rows,
        rows,
        P(),
        P(),
        P(),
        P(),
        P(),
        P(),
        P(),
        P(),
        P(None, None, LAT),
        P(LAT, None),
        P(),
        P(),
        P(),
        P(),
    )
    return jax.shard_map(
        local,
        mesh=fine,
        in_specs=placed,
        out_specs=(rows, rows),
        check_vma=False,
    )
```

```python
import functools

import jax
import jax.numpy as jnp
import numpy as np
from jax import lax
from jax.experimental import pallas as pl
from jax.experimental.pallas import tpu as pltpu
from jax.sharding import Mesh
from jax.sharding import PartitionSpec as P

HEAD = 64
G = 256
TILE = 384
NLAT = 16
LOG2E = 1.4426950408889634
SCALE = LOG2E * HEAD ** (-0.5)

AXES = ("za", "zb", "zc", "yl", "x", "yh", "core")
SIZES = (2, 2, 2, 2, 4, 2, 2)
LAT = ("yh", "core")
HEADS4 = ("zc", "yl")
KEYS4 = ("za", "zb")
OUT64 = ("zc", "yl", "x", "yh", "core")

f32 = jnp.float32
bf16 = jnp.bfloat16


def dot(a, b):
    return jnp.dot(a, b, preferred_element_type=f32)


def dot_t(a, b):
    return lax.dot_general(a, b, (((1,), (1,)), ((), ())), preferred_element_type=f32)


def norm(values, gain):
    factor = lax.rsqrt(jnp.mean(values * values, axis=-1, keepdims=True) + 1e-06)
    return (values * factor * gain).astype(bf16)


def low_lanes(rows):
    return lax.broadcasted_iota(jnp.int32, (rows, 128), 1) < HEAD


def swap(values):
    return pltpu.roll(values, HEAD, 1)


def front_kernel(
    tok_ref, lat_ref, gself_ref, gread_ref, glat_ref, gglob_ref, wqkv_hbm, wo_hbm, wkv_hbm, wq_hbm,
    mid_ref, latmid_ref, normed_ref,
    wqkv, wo, wkv, wq, packed, kv, mixed, sems,
):
    copies = [
        pltpu.make_async_copy(source, target, sems.at[i])
        for i, (source, target) in enumerate(
            ((wqkv_hbm, wqkv), (wo_hbm, wo), (wq_hbm, wq), (wkv_hbm, wkv))
        )
    ]
    for copy in copies:
        copy.start()
    groups = tok_ref.shape[0] // G
    x = tok_ref[...].astype(f32)
    normed = norm(x, gself_ref[...])
    copies[0].wait()
    packed[...] = dot(normed, wqkv[...]).astype(bf16)
    low = low_lanes(G)
    zero = jnp.zeros((G, 128), bf16)
    one = jnp.ones((G, 128), bf16)
    for g in range(groups):
        rows = slice(g * G, (g + 1) * G)
        for p in range(4):
            q2 = packed[rows, p * 128 : (p + 1) * 128]
            k2 = packed[rows, 512 + p * 128 : 512 + (p + 1) * 128]
            v2 = packed[rows, 1024 + p * 128 : 1024 + (p + 1) * 128]
            both = jnp.concatenate([jnp.where(low, q2, zero), jnp.where(low, zero, q2)], axis=0)
            s = dot_t(both, k2) * SCALE
            w = jnp.exp2(s - jnp.max(s, axis=-1, keepdims=True))
            r = dot(w.astype(bf16), jnp.concatenate([v2, one], axis=1))
            r = r[:, :128] / r[:, 128:]
            mixed[rows, p * 128 : (p + 1) * 128] = jnp.where(low, r[:G], r[G:]).astype(bf16)
    copies[1].wait()
    mid = (x + dot(mixed[...], wo[...])).astype(bf16)
    mid_ref[...] = mid
    normed = norm(mid.astype(f32), gread_ref[...])
    copies[2].wait()
    lat = lat_ref[...].astype(f32)
    query = dot(norm(lat, glat_ref[...]), wq[...]).astype(bf16)
    copies[3].wait()
    kv[...] = dot(normed, wkv[...]).astype(bf16)
    part = lax.broadcasted_iota(jnp.int32, (NLAT, 256), 1) // HEAD
    scores = []
    for g in range(groups):
        for quad in range(4):
            lanes = slice(quad * 256, (quad + 1) * 256)
            q4 = query[g * NLAT : (g + 1) * NLAT, lanes]
            stacked = jnp.concatenate(
                [jnp.where(part == a, q4, jnp.zeros_like(q4)) for a in range(4)], axis=0
            )
            scores.append(dot_t(stacked, kv[g * G : (g + 1) * G, lanes]))
    s = jnp.concatenate(scores, axis=0) * SCALE
    w = jnp.exp2(s - jnp.max(s, axis=-1, keepdims=True))
    total = jnp.sum(w, axis=-1, keepdims=True)
    w = w.astype(bf16)
    reads = []
    for g in range(groups):
        blocks = []
        for quad in range(4):
            at = slice((g * 4 + quad) * 4 * NLAT, (g * 4 + quad + 1) * 4 * NLAT)
            lanes = slice(1024 + quad * 256, 1024 + (quad + 1) * 256)
            r = dot(w[at], kv[g * G : (g + 1) * G, lanes]) / total[at]
            got = jnp.zeros((NLAT, 256), f32)
            for a in range(4):
                got = jnp.where(part == a, r[a * NLAT : (a + 1) * NLAT], got)
            blocks.append(got)
        reads.append(jnp.concatenate(blocks, axis=1))
    latmid = (lat + jnp.concatenate(reads, axis=0)).astype(bf16)
    latmid_ref[...] = latmid
    normed_ref[...] = norm(latmid.astype(f32), gglob_ref[...])


def project_kernel(block_ref, w_ref, out_ref):
    block = block_ref[...]
    rows = block.shape[0]
    half = rows // 2
    q = dot(block, w_ref[0]).astype(bf16).astype(f32)
    k = dot(block, w_ref[1]).astype(bf16).astype(f32)
    v = dot(block, w_ref[2]).astype(bf16).astype(f32)
    low = low_lanes(rows)
    lowh = low_lanes(half)
    for pair in range(2):
        lanes = slice(pair * 128, (pair + 1) * 128)
        q2, k2, v2 = q[:, lanes], k[:, lanes], v[:, lanes]
        out_ref[2 * pair, :rows] = jnp.where(low, k2, swap(v2)).astype(bf16)
        out_ref[2 * pair + 1, :rows] = jnp.where(low, swap(k2), v2).astype(bf16)
        out_ref[2 * pair, rows:] = jnp.where(lowh, q2[:half], swap(q2[half:])).astype(bf16)
        out_ref[2 * pair + 1, rows:] = jnp.where(lowh, swap(q2[:half]), q2[half:]).astype(bf16)


def unpack_queries(q_refs, starts, rows, queries):
    half = rows // 2
    low = low_lanes(half)
    for k, (ref, start) in enumerate(zip(q_refs, starts)):
        for t in range(4):
            got = ref[t, start : start + half].astype(f32)
            zero = jnp.zeros_like(got)
            at = (k * 4 + t) * rows
            both = jnp.concatenate(
                [jnp.where(low, got, zero), jnp.where(low, swap(got), zero)], axis=0
            )
            queries[at : at + rows, :] = both.astype(bf16)


def attend_part(queries, key_refs, rows, before, finish):
    keys = jnp.concatenate(
        [ref[t, :rows] for ref in key_refs for t in range(ref.shape[0])], axis=0
    )
    values = jnp.where(low_lanes(keys.shape[0]), jnp.ones_like(keys), keys)
    step = TILE
    for k in range(queries.shape[0] // step):
        at = slice(k * step, (k + 1) * step)
        s = dot_t(queries[at, :], keys) * SCALE
        peak = jnp.max(s, axis=-1, keepdims=True)
        if before is None:
            state = dot(jnp.exp2(s - peak).astype(bf16), values)
        else:
            old_peak = before[1, at, :]
            wide = jnp.maximum(peak, old_peak)
            peak = wide[:, :1]
            state = dot(jnp.exp2(s - peak).astype(bf16), values)
            state = state + before[0, at, :] * jnp.exp2(old_peak - wide)
        finish(k, state, peak)


def keep_state(state_ref):
    def keep(k, state, peak):
        state_ref[0, k * TILE : (k + 1) * TILE, :] = state
        state_ref[1, k * TILE : (k + 1) * TILE, :] = jnp.broadcast_to(peak, state.shape)

    return keep


def attend_first_kernel(own_ref, q1_ref, q2_ref, q3_ref, queries_ref, state_ref):
    rows = q1_ref.shape[1] * 2
    unpack_queries((own_ref, q1_ref, q2_ref, q3_ref), (rows, 0, 0, 0), rows, queries_ref)
    attend_part(queries_ref, (own_ref,), rows, None, keep_state(state_ref))


def attend_next_kernel(queries_ref, kv1_ref, kv2_ref, before_ref, state_ref):
    rows = kv1_ref.shape[1]
    attend_part(
        queries_ref, (kv1_ref, kv2_ref), rows, before_ref, keep_state(state_ref)
    )


def attend_last_kernel(place_ref, queries_ref, kv1_ref, kv2_ref, before_ref, out_ref):
    rows = kv1_ref.shape[1]
    unit = rows // 4
    half = unit // 2
    me = place_ref[0]
    low = low_lanes(half)
    lane = lax.broadcasted_iota(jnp.int32, (8, 128), 1)
    term = lax.rem(lane, 3)

    def send(k, state, peak):
        turned = swap(state)
        for t in range(TILE // rows):
            for u in range(4):
                at = (t * 4 + u) * unit
                top = slice(at, at + half)
                end = slice(at + half, at + unit)
                packed = jnp.where(low, turned[top], state[end]) / jnp.where(
                    low, state[top], turned[end]
                )
                sums = jnp.ones((8, 128), f32)
                peaks = jnp.zeros((8, 128), f32)
                for a in range(unit // 8):
                    here = jnp.logical_and(lane >= 3 * a, lane < 3 * a + 3)
                    part = slice(at + 8 * a, at + 8 * a + 8)
                    sums = jnp.where(here, state[part], sums)
                    peaks = jnp.where(here, peak[part], peaks)
                size = peaks + jnp.log2(sums)
                first = size.astype(bf16).astype(f32)
                second = (size - first).astype(bf16).astype(f32)
                stats = jnp.where(
                    term == 0, first, jnp.where(term == 1, second, size - first - second)
                )
                source = k * (TILE // rows) + t
                out_ref[source % 4, me ^ (source // 4), u * 32 : (u + 1) * 32] = jnp.concatenate(
                    [packed, stats], axis=0
                ).astype(bf16)

    attend_part(queries_ref, (kv1_ref, kv2_ref), rows, before_ref, send)


def write_query_kernel(mid_ref, gain_ref, w_ref, out_ref):
    out_ref[...] = dot(norm(mid_ref[...].astype(f32), gain_ref[...]), w_ref[...]).astype(bf16)


def back_kernel(
    place_ref, got_ref, latmid_ref, gwlat_ref, mid_ref, query_ref, wo0, wo1, wo2, wo3, wkv_hbm,
    tok_ref, lat_ref,
    wo, wkv, shares, sems,
):
    moves = [(source, wo.at[i]) for i, source in enumerate((wo0, wo1, wo2, wo3))]
    copies = [
        pltpu.make_async_copy(source, target, sems.at[i])
        for i, (source, target) in enumerate(moves + [(wkv_hbm, wkv)])
    ]
    for copy in copies:
        copy.start()
    me = place_ref[0]
    rows = latmid_ref.shape[0]
    half = rows // 2
    low = low_lanes(half)
    low8 = low_lanes(8)
    stats = got_ref[:, half:].astype(f32).reshape(64 * 8, 128)
    sizes = stats + pltpu.roll(stats, 127, 1) + pltpu.roll(stats, 126, 1)
    sizes = sizes.reshape(4, 4, 4, 8, 128)
    weights = jnp.exp2(sizes - jnp.max(sizes, axis=1, keepdims=True))
    weights = weights / jnp.sum(weights, axis=1, keepdims=True)
    shares[...] = weights.reshape(64, 8, 128)
    latents = latmid_ref[...].astype(f32)
    for d in range(4):
        heads = []
        for t in range(4):
            mixed = jnp.zeros((half, 128), f32)
            for x in range(4):
                source = t * 16 + x * 4 + (me ^ d)
                share = shares[source]
                spread = [
                    jnp.where(low8, share[:, 3 * b : 3 * b + 1], share[:, c : c + 1])
                    for b, c in ((b, 3 * (b + half // 8)) for b in range(half // 8))
                ]
                part = got_ref[source].astype(f32)[:half]
                mixed = mixed + part * jnp.concatenate(spread, axis=0)
            heads.append(mixed)
        pairs = []
        for one, two in ((heads[0], heads[1]), (heads[2], heads[3])):
            top = jnp.where(low, one, swap(two))
            end = jnp.where(low, swap(one), two)
            pairs.append(jnp.concatenate([top, end], axis=0).astype(bf16))
        copies[d].wait()
        latents = latents + dot(jnp.concatenate(pairs, axis=1), wo[d])
    latents = latents.astype(bf16)
    lat_ref[...] = latents
    normed = norm(latents.astype(f32), gwlat_ref[...])
    copies[4].wait()
    kv = dot(normed, wkv[...]).astype(bf16)
    head_of_row = lax.broadcasted_iota(jnp.int32, (8 * NLAT, 512), 0) // NLAT
    head_of_lane = lax.broadcasted_iota(jnp.int32, (8 * NLAT, 512), 1) // HEAD
    here = head_of_row == head_of_lane
    ones = jnp.where(here, 1.0, 0.0).astype(bf16)
    groups = rows // NLAT
    zero = jnp.zeros((8 * NLAT, 512), bf16)
    scores, values = [], []
    for g in range(groups):
        k = kv[g * NLAT : (g + 1) * NLAT, :512]
        v = kv[g * NLAT : (g + 1) * NLAT, 512:]
        k8 = jnp.where(here, jnp.concatenate([k] * 8, axis=0), zero)
        v8 = jnp.where(here, jnp.concatenate([v] * 8, axis=0), zero)
        values.append(jnp.concatenate([v8, ones], axis=1))
        scores.append(dot_t(k8, query_ref[g * G : (g + 1) * G, :]))
    s = (jnp.concatenate(scores, axis=1) * SCALE).reshape(8, NLAT, groups * G)
    w = jnp.exp2(s - jnp.max(s, axis=1, keepdims=True)).reshape(8 * NLAT, groups * G)
    turned = w.astype(bf16).T
    for g in range(groups):
        at = slice(g * G, (g + 1) * G)
        written = dot(turned[at], values[g])
        tok_ref[at, :] = (
            mid_ref[at, :].astype(f32) + written[:, :512] / written[:, 512:]
        ).astype(bf16)


def params(megabytes):
    return pltpu.CompilerParams(vmem_limit_bytes=megabytes * 1024 * 1024)


def cost(flops, bytes_accessed, transcendentals=0):
    return pl.CostEstimate(
        flops=int(flops), bytes_accessed=int(bytes_accessed), transcendentals=int(transcendentals)
    )


def local(
    tokens,
    latents,
    gain_self,
    w_qkv_tok,
    w_o_tok,
    gain_read,
    w_kv_read,
    gain_lat,
    w_q_read,
    gain_glob,
    w_qkv_glob,
    w_o_glob,
    gain_write,
    w_q_write,
    gain_wlat,
    w_kv_write,
):
    token_rows, width = tokens.shape
    lat_rows, lat_width = latents.shape
    row = lambda gain: gain.reshape(1, -1)
    other = [(0, 1), (1, 0)]
    w_o_core = lax.ppermute(w_o_glob, "core", other)
    w_o_yh = lax.ppermute(w_o_glob, "yh", other)
    vmem = pl.BlockSpec(memory_space=pltpu.VMEM)
    hbm = pl.BlockSpec(memory_space=pl.ANY)
    weights = (w_qkv_tok, w_o_tok, w_kv_read, w_q_read)
    tokens_mid, latents_mid, normed = pl.pallas_call(
        front_kernel,
        in_specs=[vmem] * 6 + [hbm] * 4,
        out_specs=[vmem] * 3,
        out_shape=[
            jax.ShapeDtypeStruct(tokens.shape, bf16),
            jax.ShapeDtypeStruct(latents.shape, bf16),
            jax.ShapeDtypeStruct(latents.shape, bf16),
        ],
        scratch_shapes=[pltpu.VMEM(w.shape, bf16) for w in weights]
        + [
            pltpu.VMEM((token_rows, w_qkv_tok.shape[1]), bf16),
            pltpu.VMEM((token_rows, w_kv_read.shape[1]), bf16),
            pltpu.VMEM((token_rows, width), bf16),
            pltpu.SemaphoreType.DMA((4,)),
        ],
        compiler_params=params(60),
        name="front",
    )(
        tokens, latents, row(gain_self), row(gain_read), row(gain_lat), row(gain_glob), *weights
    )

    block = lax.all_gather(normed, LAT, axis=0, tiled=True)
    block_rows = block.shape[0]
    half = block_rows // 2
    sent = pl.pallas_call(
        project_kernel,
        in_specs=[vmem] * 2,
        out_specs=vmem,
        out_shape=jax.ShapeDtypeStruct((4, block_rows + half, 128), bf16),
        compiler_params=params(32),
        name="project",
    )(block, w_qkv_glob)
    own = lax.all_to_all(sent, HEADS4, 0, 0, tiled=True)
    own_kv = own[:, :block_rows]
    own_q = own[:, block_rows:]
    others_q = [lax.ppermute(own_q, "x", [(i, i ^ k) for i in range(4)]) for k in (1, 2, 3)]
    ahead = [(i, (i + 1) % 4) for i in range(4)]
    behind = [(i, (i - 1) % 4) for i in range(4)]
    kv_ahead = lax.ppermute(own_kv, KEYS4, ahead)
    kv_behind = lax.ppermute(own_kv, KEYS4, behind)
    kv_far1 = lax.ppermute(kv_ahead[:2], KEYS4, ahead)
    kv_far2 = lax.ppermute(kv_behind[2:], KEYS4, behind)
    place = lax.axis_index("x").astype(jnp.int32).reshape(1)
    many = 16 * block_rows

    def part_cost(parts):
        return cost(parts * many * many * 64, many * 128 * 10, parts * many * many // 4)

    queries, state = pl.pallas_call(
        attend_first_kernel,
        in_specs=[vmem] * 4,
        out_specs=[vmem] * 2,
        out_shape=[
            jax.ShapeDtypeStruct((many, 128), bf16),
            jax.ShapeDtypeStruct((2, many, 128), f32),
        ],
        compiler_params=params(32),
        cost_estimate=part_cost(1),
        name="attend_first",
    )(own, *others_q)
    state = pl.pallas_call(
        attend_next_kernel,
        in_specs=[vmem] * 4,
        out_specs=vmem,
        out_shape=jax.ShapeDtypeStruct((2, many, 128), f32),
        compiler_params=params(32),
        cost_estimate=part_cost(2),
        name="attend_next",
    )(queries, kv_ahead, kv_behind, state)
    message = 2 * lat_rows // 3
    partial = pl.pallas_call(
        attend_last_kernel,
        in_specs=[pl.BlockSpec(memory_space=pltpu.SMEM)] + [vmem] * 4,
        out_specs=vmem,
        out_shape=jax.ShapeDtypeStruct((4, 4, 4 * message, 128), bf16),
        compiler_params=params(32),
        cost_estimate=part_cost(1),
        name="attend_last",
    )(place, queries, kv_far1, kv_far2, state)
    got = lax.all_to_all(partial.reshape(64, message, 128), OUT64, 0, 0, tiled=True)
    tokens_late, w_o_late, partial = lax.optimization_barrier((tokens_mid, w_o_yh, partial))
    w_o_both = lax.ppermute(w_o_late, "core", other)
    query = pl.pallas_call(
        write_query_kernel,
        in_specs=[vmem] * 3,
        out_specs=vmem,
        out_shape=jax.ShapeDtypeStruct(tokens.shape, bf16),
        compiler_params=params(32),
        cost_estimate=cost(2 * token_rows * width * width, token_rows * width * 4),
        name="write_query",
    )(tokens_late, row(gain_write), w_q_write)
    tokens_out, latents_out = pl.pallas_call(
        back_kernel,
        in_specs=[pl.BlockSpec(memory_space=pltpu.SMEM)] + [vmem] * 5 + [hbm] * 5,
        out_specs=[vmem] * 2,
        out_shape=[
            jax.ShapeDtypeStruct(tokens.shape, bf16),
            jax.ShapeDtypeStruct(latents.shape, bf16),
        ],
        scratch_shapes=[
            pltpu.VMEM((4,) + w_o_glob.shape, bf16),
            pltpu.VMEM(w_kv_write.shape, bf16),
            pltpu.VMEM((64, 8, 128), f32),
            pltpu.SemaphoreType.DMA((5,)),
        ],
        compiler_params=params(49),
        name="back",
    )(
        lax.axis_index(LAT).astype(jnp.int32).reshape(1),
        got,
        latents_mid,
        row(gain_wlat),
        tokens_late,
        query,
        w_o_glob,
        w_o_core,
        w_o_late,
        w_o_both,
        w_kv_write,
    )
    return (tokens_out, latents_out)


def solution(mesh):
    fine = Mesh(np.asarray(mesh.devices).reshape(SIZES), AXES)
    rows = P(AXES, None)
    placed = (
        rows,
        rows,
        P(),
        P(),
        P(),
        P(),
        P(),
        P(),
        P(),
        P(),
        P(None, None, LAT),
        P(LAT, None),
        P(),
        P(),
        P(),
        P(),
    )
    return jax.shard_map(
        local,
        mesh=fine,
        in_specs=placed,
        out_specs=(rows, rows),
        check_vma=False,
    )
```

```python
import functools

import jax
import jax.numpy as jnp
import numpy as np
from jax import lax
from jax.experimental import pallas as pl
from jax.experimental.pallas import tpu as pltpu
from jax.sharding import Mesh
from jax.sharding import PartitionSpec as P

HEAD = 64
G = 256
TILE = 384
NLAT = 16
LOG2E = 1.4426950408889634
SCALE = LOG2E * HEAD ** (-0.5)

AXES = ("za", "zb", "zc", "yl", "x", "yh", "core")
SIZES = (2, 2, 2, 2, 4, 2, 2)
LAT = ("yh", "core")
HEADS4 = ("zc", "yl")
KEYS4 = ("za", "zb")
OUT64 = ("zc", "yl", "x", "yh", "core")

f32 = jnp.float32
bf16 = jnp.bfloat16


def dot(a, b):
    return jnp.dot(a, b, preferred_element_type=f32)


def dot_t(a, b):
    return lax.dot_general(a, b, (((1,), (1,)), ((), ())), preferred_element_type=f32)


def norm(values, gain):
    factor = lax.rsqrt(jnp.mean(values * values, axis=-1, keepdims=True) + 1e-06)
    return (values * factor * gain).astype(bf16)


def low_lanes(rows):
    return lax.broadcasted_iota(jnp.int32, (rows, 128), 1) < HEAD


def swap(values):
    return pltpu.roll(values, HEAD, 1)


def front_kernel(
    tok_ref, lat_ref, gself_ref, gread_ref, glat_ref, gglob_ref, wqkv_hbm, wo_hbm, wkv_hbm, wq_hbm,
    mid_ref, latmid_ref, normed_ref,
    wqkv, wo, wkv, wq, packed, kv, mixed, sems,
):
    copies = [
        pltpu.make_async_copy(source, target, sems.at[i])
        for i, (source, target) in enumerate(
            ((wqkv_hbm, wqkv), (wo_hbm, wo), (wq_hbm, wq), (wkv_hbm, wkv))
        )
    ]
    for copy in copies:
        copy.start()
    groups = tok_ref.shape[0] // G
    x = tok_ref[...].astype(f32)
    normed = norm(x, gself_ref[...])
    copies[0].wait()
    packed[...] = dot(normed, wqkv[...]).astype(bf16)
    low = low_lanes(G)
    zero = jnp.zeros((G, 128), bf16)
    one = jnp.ones((G, 128), bf16)
    for g in range(groups):
        rows = slice(g * G, (g + 1) * G)
        for p in range(4):
            q2 = packed[rows, p * 128 : (p + 1) * 128]
            k2 = packed[rows, 512 + p * 128 : 512 + (p + 1) * 128]
            v2 = packed[rows, 1024 + p * 128 : 1024 + (p + 1) * 128]
            both = jnp.concatenate([jnp.where(low, q2, zero), jnp.where(low, zero, q2)], axis=0)
            s = dot_t(both, k2) * SCALE
            w = jnp.exp2(s - jnp.max(s, axis=-1, keepdims=True))
            r = dot(w.astype(bf16), jnp.concatenate([v2, one], axis=1))
            r = r[:, :128] / r[:, 128:]
            mixed[rows, p * 128 : (p + 1) * 128] = jnp.where(low, r[:G], r[G:]).astype(bf16)
    copies[1].wait()
    mid = (x + dot(mixed[...], wo[...])).astype(bf16)
    mid_ref[...] = mid
    normed = norm(mid.astype(f32), gread_ref[...])
    copies[2].wait()
    lat = lat_ref[...].astype(f32)
    query = dot(norm(lat, glat_ref[...]), wq[...]).astype(bf16)
    copies[3].wait()
    kv[...] = dot(normed, wkv[...]).astype(bf16)
    part = lax.broadcasted_iota(jnp.int32, (NLAT, 256), 1) // HEAD
    scores = []
    for g in range(groups):
        for quad in range(4):
            lanes = slice(quad * 256, (quad + 1) * 256)
            q4 = query[g * NLAT : (g + 1) * NLAT, lanes]
            stacked = jnp.concatenate(
                [jnp.where(part == a, q4, jnp.zeros_like(q4)) for a in range(4)], axis=0
            )
            scores.append(dot_t(stacked, kv[g * G : (g + 1) * G, lanes]))
    s = jnp.concatenate(scores, axis=0) * SCALE
    w = jnp.exp2(s - jnp.max(s, axis=-1, keepdims=True))
    total = jnp.sum(w, axis=-1, keepdims=True)
    w = w.astype(bf16)
    reads = []
    for g in range(groups):
        blocks = []
        for quad in range(4):
            at = slice((g * 4 + quad) * 4 * NLAT, (g * 4 + quad + 1) * 4 * NLAT)
            lanes = slice(1024 + quad * 256, 1024 + (quad + 1) * 256)
            r = dot(w[at], kv[g * G : (g + 1) * G, lanes]) / total[at]
            got = jnp.zeros((NLAT, 256), f32)
            for a in range(4):
                got = jnp.where(part == a, r[a * NLAT : (a + 1) * NLAT], got)
            blocks.append(got)
        reads.append(jnp.concatenate(blocks, axis=1))
    latmid = (lat + jnp.concatenate(reads, axis=0)).astype(bf16)
    latmid_ref[...] = latmid
    normed_ref[...] = norm(latmid.astype(f32), gglob_ref[...])


def project_kernel(block_ref, w_ref, out_ref):
    block = block_ref[...]
    rows = block.shape[0]
    half = rows // 2
    q = dot(block, w_ref[0]).astype(bf16).astype(f32)
    k = dot(block, w_ref[1]).astype(bf16).astype(f32)
    v = dot(block, w_ref[2]).astype(bf16).astype(f32)
    low = low_lanes(rows)
    lowh = low_lanes(half)
    for pair in range(2):
        lanes = slice(pair * 128, (pair + 1) * 128)
        q2, k2, v2 = q[:, lanes], k[:, lanes], v[:, lanes]
        out_ref[2 * pair, :rows] = jnp.where(low, k2, swap(v2)).astype(bf16)
        out_ref[2 * pair + 1, :rows] = jnp.where(low, swap(k2), v2).astype(bf16)
        out_ref[2 * pair, rows:] = jnp.where(lowh, q2[:half], swap(q2[half:])).astype(bf16)
        out_ref[2 * pair + 1, rows:] = jnp.where(lowh, swap(q2[:half]), q2[half:]).astype(bf16)


def unpack_queries(q_refs, starts, rows, queries):
    half = rows // 2
    low = low_lanes(half)
    for k, (ref, start) in enumerate(zip(q_refs, starts)):
        for t in range(4):
            got = ref[t, start : start + half].astype(f32)
            zero = jnp.zeros_like(got)
            at = (k * 4 + t) * rows
            both = jnp.concatenate(
                [jnp.where(low, got, zero), jnp.where(low, swap(got), zero)], axis=0
            )
            queries[at : at + rows, :] = both.astype(bf16)


def attend_part(queries, key_refs, rows, before, finish, exact=True):
    keys = jnp.concatenate(
        [ref[t, :rows] for ref in key_refs for t in range(ref.shape[0])], axis=0
    )
    values = jnp.where(low_lanes(keys.shape[0]), jnp.ones_like(keys), keys)
    step = TILE
    worst = None
    for k in range(queries.shape[0] // step):
        at = slice(k * step, (k + 1) * step)
        s = dot_t(queries[at, :], keys) * SCALE
        if before is None:
            peak = jnp.max(s, axis=-1, keepdims=True)
            state = dot(jnp.exp2(s - peak).astype(bf16), values)
        elif not exact:
            peak = before[1, at, :]
            shift = jnp.concatenate([peak] * (keys.shape[0] // 128), axis=1)
            state = dot(jnp.exp2(s - shift).astype(bf16), values) + before[0, at, :]
            worst = state if worst is None else jnp.maximum(worst, state)
        else:
            old_peak = before[1, at, :]
            peak = jnp.max(s, axis=-1, keepdims=True)
            wide = jnp.maximum(peak, old_peak)
            peak = wide[:, :1]
            state = dot(jnp.exp2(s - peak).astype(bf16), values)
            state = state + before[0, at, :] * jnp.exp2(old_peak - wide)
        finish(k, state, peak)
    if not exact:
        return jnp.max(jnp.where(low_lanes(step), worst, 0.0))


def attend_more(queries, key_refs, rows, before, finish):
    largest = attend_part(queries, key_refs, rows, before, finish, exact=False)

    @pl.when(jnp.logical_not(largest < 2.0**90))
    def _():
        attend_part(queries, key_refs, rows, before, finish)


def keep_state(state_ref):
    def keep(k, state, peak):
        state_ref[0, k * TILE : (k + 1) * TILE, :] = state
        state_ref[1, k * TILE : (k + 1) * TILE, :] = jnp.broadcast_to(peak, state.shape)

    return keep


def attend_first_kernel(own_ref, q1_ref, q2_ref, q3_ref, queries_ref, state_ref):
    rows = q1_ref.shape[1] * 2
    unpack_queries((own_ref, q1_ref, q2_ref, q3_ref), (rows, 0, 0, 0), rows, queries_ref)
    attend_part(queries_ref, (own_ref,), rows, None, keep_state(state_ref))


def attend_next_kernel(queries_ref, kv1_ref, kv2_ref, before_ref, state_ref):
    rows = kv1_ref.shape[1]
    attend_more(queries_ref, (kv1_ref, kv2_ref), rows, before_ref, keep_state(state_ref))


def attend_last_kernel(place_ref, queries_ref, kv1_ref, kv2_ref, before_ref, out_ref):
    rows = kv1_ref.shape[1]
    unit = rows // 4
    half = unit // 2
    me = place_ref[0]
    low = low_lanes(half)
    lane = lax.broadcasted_iota(jnp.int32, (8, 128), 1)
    term = lax.rem(lane, 3)

    def send(k, state, peak):
        turned = swap(state)
        for t in range(TILE // rows):
            for u in range(4):
                at = (t * 4 + u) * unit
                top = slice(at, at + half)
                end = slice(at + half, at + unit)
                packed = jnp.where(low, turned[top], state[end]) / jnp.where(
                    low, state[top], turned[end]
                )
                sums = jnp.ones((8, 128), f32)
                peaks = jnp.zeros((8, 128), f32)
                for a in range(unit // 8):
                    here = jnp.logical_and(lane >= 3 * a, lane < 3 * a + 3)
                    part = slice(at + 8 * a, at + 8 * a + 8)
                    sums = jnp.where(here, state[part], sums)
                    peaks = jnp.where(here, peak[part], peaks)
                size = peaks + jnp.log2(sums)
                first = size.astype(bf16).astype(f32)
                second = (size - first).astype(bf16).astype(f32)
                stats = jnp.where(
                    term == 0, first, jnp.where(term == 1, second, size - first - second)
                )
                source = k * (TILE // rows) + t
                out_ref[source % 4, me ^ (source // 4), u * 32 : (u + 1) * 32] = jnp.concatenate(
                    [packed, stats], axis=0
                ).astype(bf16)

    attend_part(queries_ref, (kv1_ref, kv2_ref), rows, before_ref, send)


def write_query_kernel(mid_ref, gain_ref, w_ref, out_ref):
    out_ref[...] = dot(norm(mid_ref[...].astype(f32), gain_ref[...]), w_ref[...]).astype(bf16)


def back_kernel(
    place_ref, got_ref, latmid_ref, gwlat_ref, mid_ref, query_ref, wo0, wo1, wo2, wo3, wkv_hbm,
    tok_ref, lat_ref,
    wo, wkv, shares, sems,
):
    moves = [(source, wo.at[i]) for i, source in enumerate((wo0, wo1, wo2, wo3))]
    copies = [
        pltpu.make_async_copy(source, target, sems.at[i])
        for i, (source, target) in enumerate(moves + [(wkv_hbm, wkv)])
    ]
    for copy in copies:
        copy.start()
    me = place_ref[0]
    rows = latmid_ref.shape[0]
    half = rows // 2
    low = low_lanes(half)
    low8 = low_lanes(8)
    stats = got_ref[:, half:].astype(f32).reshape(64 * 8, 128)
    sizes = stats + pltpu.roll(stats, 127, 1) + pltpu.roll(stats, 126, 1)
    sizes = sizes.reshape(4, 4, 4, 8, 128)
    weights = jnp.exp2(sizes - jnp.max(sizes, axis=1, keepdims=True))
    weights = weights / jnp.sum(weights, axis=1, keepdims=True)
    shares[...] = weights.reshape(64, 8, 128)
    latents = latmid_ref[...].astype(f32)
    for d in range(4):
        heads = []
        for t in range(4):
            mixed = jnp.zeros((half, 128), f32)
            for x in range(4):
                source = t * 16 + x * 4 + (me ^ d)
                share = shares[source]
                spread = [
                    jnp.where(low8, share[:, 3 * b : 3 * b + 1], share[:, c : c + 1])
                    for b, c in ((b, 3 * (b + half // 8)) for b in range(half // 8))
                ]
                part = got_ref[source].astype(f32)[:half]
                mixed = mixed + part * jnp.concatenate(spread, axis=0)
            heads.append(mixed)
        pairs = []
        for one, two in ((heads[0], heads[1]), (heads[2], heads[3])):
            top = jnp.where(low, one, swap(two))
            end = jnp.where(low, swap(one), two)
            pairs.append(jnp.concatenate([top, end], axis=0).astype(bf16))
        copies[d].wait()
        latents = latents + dot(jnp.concatenate(pairs, axis=1), wo[d])
    latents = latents.astype(bf16)
    lat_ref[...] = latents
    normed = norm(latents.astype(f32), gwlat_ref[...])
    copies[4].wait()
    kv = dot(normed, wkv[...]).astype(bf16)
    head_of_row = lax.broadcasted_iota(jnp.int32, (8 * NLAT, 512), 0) // NLAT
    head_of_lane = lax.broadcasted_iota(jnp.int32, (8 * NLAT, 512), 1) // HEAD
    here = head_of_row == head_of_lane
    ones = jnp.where(here, 1.0, 0.0).astype(bf16)
    groups = rows // NLAT
    zero = jnp.zeros((8 * NLAT, 512), bf16)
    scores, values = [], []
    for g in range(groups):
        k = kv[g * NLAT : (g + 1) * NLAT, :512]
        v = kv[g * NLAT : (g + 1) * NLAT, 512:]
        k8 = jnp.where(here, jnp.concatenate([k] * 8, axis=0), zero)
        v8 = jnp.where(here, jnp.concatenate([v] * 8, axis=0), zero)
        values.append(jnp.concatenate([v8, ones], axis=1))
        scores.append(dot_t(k8, query_ref[g * G : (g + 1) * G, :]))
    s = (jnp.concatenate(scores, axis=1) * SCALE).reshape(8, NLAT, groups * G)
    w = jnp.exp2(s - jnp.max(s, axis=1, keepdims=True)).reshape(8 * NLAT, groups * G)
    turned = w.astype(bf16).T
    for g in range(groups):
        at = slice(g * G, (g + 1) * G)
        written = dot(turned[at], values[g])
        tok_ref[at, :] = (
            mid_ref[at, :].astype(f32) + written[:, :512] / written[:, 512:]
        ).astype(bf16)


def params(megabytes):
    return pltpu.CompilerParams(vmem_limit_bytes=megabytes * 1024 * 1024)


def cost(flops, bytes_accessed, transcendentals=0):
    return pl.CostEstimate(
        flops=int(flops), bytes_accessed=int(bytes_accessed), transcendentals=int(transcendentals)
    )


def local(
    tokens,
    latents,
    gain_self,
    w_qkv_tok,
    w_o_tok,
    gain_read,
    w_kv_read,
    gain_lat,
    w_q_read,
    gain_glob,
    w_qkv_glob,
    w_o_glob,
    gain_write,
    w_q_write,
    gain_wlat,
    w_kv_write,
):
    token_rows, width = tokens.shape
    lat_rows, lat_width = latents.shape
    row = lambda gain: gain.reshape(1, -1)
    other = [(0, 1), (1, 0)]
    w_o_core = lax.ppermute(w_o_glob, "core", other)
    w_o_yh = lax.ppermute(w_o_glob, "yh", other)
    vmem = pl.BlockSpec(memory_space=pltpu.VMEM)
    hbm = pl.BlockSpec(memory_space=pl.ANY)
    weights = (w_qkv_tok, w_o_tok, w_kv_read, w_q_read)
    tokens_mid, latents_mid, normed = pl.pallas_call(
        front_kernel,
        in_specs=[vmem] * 6 + [hbm] * 4,
        out_specs=[vmem] * 3,
        out_shape=[
            jax.ShapeDtypeStruct(tokens.shape, bf16),
            jax.ShapeDtypeStruct(latents.shape, bf16),
            jax.ShapeDtypeStruct(latents.shape, bf16),
        ],
        scratch_shapes=[pltpu.VMEM(w.shape, bf16) for w in weights]
        + [
            pltpu.VMEM((token_rows, w_qkv_tok.shape[1]), bf16),
            pltpu.VMEM((token_rows, w_kv_read.shape[1]), bf16),
            pltpu.VMEM((token_rows, width), bf16),
            pltpu.SemaphoreType.DMA((4,)),
        ],
        compiler_params=params(60),
        name="front",
    )(
        tokens, latents, row(gain_self), row(gain_read), row(gain_lat), row(gain_glob), *weights
    )

    block = lax.all_gather(normed, LAT, axis=0, tiled=True)
    block_rows = block.shape[0]
    half = block_rows // 2
    sent = pl.pallas_call(
        project_kernel,
        in_specs=[vmem] * 2,
        out_specs=vmem,
        out_shape=jax.ShapeDtypeStruct((4, block_rows + half, 128), bf16),
        compiler_params=params(32),
        name="project",
    )(block, w_qkv_glob)
    own = lax.all_to_all(sent, HEADS4, 0, 0, tiled=True)
    own_kv = own[:, :block_rows]
    own_q = own[:, block_rows:]
    others_q = [lax.ppermute(own_q, "x", [(i, i ^ k) for i in range(4)]) for k in (1, 2, 3)]
    ahead = [(i, (i + 1) % 4) for i in range(4)]
    behind = [(i, (i - 1) % 4) for i in range(4)]
    kv_ahead = lax.ppermute(own_kv, KEYS4, ahead)
    kv_behind = lax.ppermute(own_kv, KEYS4, behind)
    kv_far1 = lax.ppermute(kv_ahead[:2], KEYS4, ahead)
    kv_far2 = lax.ppermute(kv_behind[2:], KEYS4, behind)
    place = lax.axis_index("x").astype(jnp.int32).reshape(1)
    many = 16 * block_rows

    def part_cost(parts):
        return cost(parts * many * many * 64, many * 128 * 10, parts * many * many // 4)

    queries, state = pl.pallas_call(
        attend_first_kernel,
        in_specs=[vmem] * 4,
        out_specs=[vmem] * 2,
        out_shape=[
            jax.ShapeDtypeStruct((many, 128), bf16),
            jax.ShapeDtypeStruct((2, many, 128), f32),
        ],
        compiler_params=params(32),
        cost_estimate=part_cost(1),
        name="attend_first",
    )(own, *others_q)
    state = pl.pallas_call(
        attend_next_kernel,
        in_specs=[vmem] * 4,
        out_specs=vmem,
        out_shape=jax.ShapeDtypeStruct((2, many, 128), f32),
        compiler_params=params(32),
        cost_estimate=part_cost(2),
        name="attend_next",
    )(queries, kv_ahead, kv_behind, state)
    message = 2 * lat_rows // 3
    partial = pl.pallas_call(
        attend_last_kernel,
        in_specs=[pl.BlockSpec(memory_space=pltpu.SMEM)] + [vmem] * 4,
        out_specs=vmem,
        out_shape=jax.ShapeDtypeStruct((4, 4, 4 * message, 128), bf16),
        compiler_params=params(32),
        cost_estimate=part_cost(1),
        name="attend_last",
    )(place, queries, kv_far1, kv_far2, state)
    got = lax.all_to_all(partial.reshape(64, message, 128), OUT64, 0, 0, tiled=True)
    tokens_late, w_o_late, partial = lax.optimization_barrier((tokens_mid, w_o_yh, partial))
    w_o_both = lax.ppermute(w_o_late, "core", other)
    query = pl.pallas_call(
        write_query_kernel,
        in_specs=[vmem] * 3,
        out_specs=vmem,
        out_shape=jax.ShapeDtypeStruct(tokens.shape, bf16),
        compiler_params=params(32),
        cost_estimate=cost(2 * token_rows * width * width, token_rows * width * 4),
        name="write_query",
    )(tokens_late, row(gain_write), w_q_write)
    tokens_out, latents_out = pl.pallas_call(
        back_kernel,
        in_specs=[pl.BlockSpec(memory_space=pltpu.SMEM)] + [vmem] * 5 + [hbm] * 5,
        out_specs=[vmem] * 2,
        out_shape=[
            jax.ShapeDtypeStruct(tokens.shape, bf16),
            jax.ShapeDtypeStruct(latents.shape, bf16),
        ],
        scratch_shapes=[
            pltpu.VMEM((4,) + w_o_glob.shape, bf16),
            pltpu.VMEM(w_kv_write.shape, bf16),
            pltpu.VMEM((64, 8, 128), f32),
            pltpu.SemaphoreType.DMA((5,)),
        ],
        compiler_params=params(49),
        name="back",
    )(
        lax.axis_index(LAT).astype(jnp.int32).reshape(1),
        got,
        latents_mid,
        row(gain_wlat),
        tokens_late,
        query,
        w_o_glob,
        w_o_core,
        w_o_late,
        w_o_both,
        w_kv_write,
    )
    return (tokens_out, latents_out)


def solution(mesh):
    fine = Mesh(np.asarray(mesh.devices).reshape(SIZES), AXES)
    rows = P(AXES, None)
    placed = (
        rows,
        rows,
        P(),
        P(),
        P(),
        P(),
        P(),
        P(),
        P(),
        P(),
        P(None, None, LAT),
        P(LAT, None),
        P(),
        P(),
        P(),
        P(),
    )
    return jax.shard_map(
        local,
        mesh=fine,
        in_specs=placed,
        out_specs=(rows, rows),
        check_vma=False,
    )
```

```python
import functools

import jax
import jax.numpy as jnp
import numpy as np
from jax import lax
from jax.experimental import pallas as pl
from jax.experimental.pallas import tpu as pltpu
from jax.sharding import Mesh
from jax.sharding import PartitionSpec as P

HEAD = 64
G = 256
TILE = 384
NLAT = 16
LOG2E = 1.4426950408889634
SCALE = LOG2E * HEAD ** (-0.5)

AXES = ("za", "zb", "zc", "yl", "x", "yh", "core")
SIZES = (2, 2, 2, 2, 4, 2, 2)
LAT = ("yh", "core")
HEADS4 = ("zc", "yl")
KEYS4 = ("za", "zb")
OUT64 = ("zc", "yl", "x", "yh", "core")

f32 = jnp.float32
bf16 = jnp.bfloat16


def dot(a, b):
    return jnp.dot(a, b, preferred_element_type=f32)


def dot_t(a, b):
    return lax.dot_general(a, b, (((1,), (1,)), ((), ())), preferred_element_type=f32)


def norm(values, gain):
    factor = lax.rsqrt(jnp.mean(values * values, axis=-1, keepdims=True) + 1e-06)
    return (values * factor * gain).astype(bf16)


def low_lanes(rows):
    return lax.broadcasted_iota(jnp.int32, (rows, 128), 1) < HEAD


def swap(values):
    return pltpu.roll(values, HEAD, 1)


def front_kernel(
    tok_ref, lat_ref, gself_ref, gread_ref, glat_ref, gglob_ref, wqkv_hbm, wo_hbm, wkv_hbm, wq_hbm,
    mid_ref, latmid_ref, normed_ref,
    wqkv, wo, wkv, wq, packed, kv, mixed, sems,
):
    copies = [
        pltpu.make_async_copy(source, target, sems.at[i])
        for i, (source, target) in enumerate(
            ((wqkv_hbm, wqkv), (wo_hbm, wo), (wq_hbm, wq), (wkv_hbm, wkv))
        )
    ]
    for copy in copies:
        copy.start()
    groups = tok_ref.shape[0] // G
    x = tok_ref[...].astype(f32)
    normed = norm(x, gself_ref[...])
    copies[0].wait()
    packed[...] = dot(normed, wqkv[...]).astype(bf16)
    low = low_lanes(G)
    zero = jnp.zeros((G, 128), bf16)
    one = jnp.ones((G, 128), bf16)
    for g in range(groups):
        rows = slice(g * G, (g + 1) * G)
        for p in range(4):
            q2 = packed[rows, p * 128 : (p + 1) * 128]
            k2 = packed[rows, 512 + p * 128 : 512 + (p + 1) * 128]
            v2 = packed[rows, 1024 + p * 128 : 1024 + (p + 1) * 128]
            both = jnp.concatenate([jnp.where(low, q2, zero), jnp.where(low, zero, q2)], axis=0)
            s = dot_t(both, k2) * SCALE
            w = jnp.exp2(s - jnp.max(s, axis=-1, keepdims=True))
            r = dot(w.astype(bf16), jnp.concatenate([v2, one], axis=1))
            r = r[:, :128] / r[:, 128:]
            mixed[rows, p * 128 : (p + 1) * 128] = jnp.where(low, r[:G], r[G:]).astype(bf16)
    copies[1].wait()
    mid = (x + dot(mixed[...], wo[...])).astype(bf16)
    mid_ref[...] = mid
    normed = norm(mid.astype(f32), gread_ref[...])
    copies[2].wait()
    lat = lat_ref[...].astype(f32)
    query = dot(norm(lat, glat_ref[...]), wq[...]).astype(bf16)
    copies[3].wait()
    kv[...] = dot(normed, wkv[...]).astype(bf16)
    part = lax.broadcasted_iota(jnp.int32, (NLAT, 256), 1) // HEAD
    scores = []
    for g in range(groups):
        for quad in range(4):
            lanes = slice(quad * 256, (quad + 1) * 256)
            q4 = query[g * NLAT : (g + 1) * NLAT, lanes]
            stacked = jnp.concatenate(
                [jnp.where(part == a, q4, jnp.zeros_like(q4)) for a in range(4)], axis=0
            )
            scores.append(dot_t(stacked, kv[g * G : (g + 1) * G, lanes]))
    s = jnp.concatenate(scores, axis=0) * SCALE
    w = jnp.exp2(s - jnp.max(s, axis=-1, keepdims=True))
    total = jnp.sum(w, axis=-1, keepdims=True)
    w = w.astype(bf16)
    reads = []
    for g in range(groups):
        blocks = []
        for quad in range(4):
            at = slice((g * 4 + quad) * 4 * NLAT, (g * 4 + quad + 1) * 4 * NLAT)
            lanes = slice(1024 + quad * 256, 1024 + (quad + 1) * 256)
            r = dot(w[at], kv[g * G : (g + 1) * G, lanes]) / total[at]
            got = jnp.zeros((NLAT, 256), f32)
            for a in range(4):
                got = jnp.where(part == a, r[a * NLAT : (a + 1) * NLAT], got)
            blocks.append(got)
        reads.append(jnp.concatenate(blocks, axis=1))
    latmid = (lat + jnp.concatenate(reads, axis=0)).astype(bf16)
    latmid_ref[...] = latmid
    normed_ref[...] = norm(latmid.astype(f32), gglob_ref[...])


def project_kernel(block_ref, w_ref, out_ref):
    block = block_ref[...]
    rows = block.shape[0]
    half = rows // 2
    q = dot(block, w_ref[0]).astype(bf16).astype(f32)
    k = dot(block, w_ref[1]).astype(bf16).astype(f32)
    v = dot(block, w_ref[2]).astype(bf16).astype(f32)
    low = low_lanes(rows)
    lowh = low_lanes(half)
    for pair in range(2):
        lanes = slice(pair * 128, (pair + 1) * 128)
        q2, k2, v2 = q[:, lanes], k[:, lanes], v[:, lanes]
        out_ref[2 * pair, :rows] = jnp.where(low, k2, swap(v2)).astype(bf16)
        out_ref[2 * pair + 1, :rows] = jnp.where(low, swap(k2), v2).astype(bf16)
        out_ref[2 * pair, rows:] = jnp.where(lowh, q2[:half], swap(q2[half:])).astype(bf16)
        out_ref[2 * pair + 1, rows:] = jnp.where(lowh, swap(q2[:half]), q2[half:]).astype(bf16)


def unpack_queries(q_refs, starts, rows, queries):
    half = rows // 2
    low = low_lanes(half)
    for k, (ref, start) in enumerate(zip(q_refs, starts)):
        for t in range(4):
            got = ref[t, start : start + half].astype(f32)
            zero = jnp.zeros_like(got)
            at = (k * 4 + t) * rows
            both = jnp.concatenate(
                [jnp.where(low, got, zero), jnp.where(low, swap(got), zero)], axis=0
            )
            queries[at : at + rows, :] = both.astype(bf16)


def attend_part(queries, key_refs, rows, before, finish, exact=True, loop=False):
    keys = jnp.concatenate(
        [ref[t, :rows] for ref in key_refs for t in range(ref.shape[0])], axis=0
    )
    values = jnp.where(low_lanes(keys.shape[0]), jnp.ones_like(keys), keys)
    steps = queries.shape[0] // TILE
    worst = None

    def step(k):
        at = pl.ds(pl.multiple_of(k * TILE, TILE), TILE) if loop else slice(k * TILE, (k + 1) * TILE)
        s = dot_t(queries[at, :], keys) * SCALE
        if before is None:
            peak = jnp.max(s, axis=-1, keepdims=True)
            state = dot(jnp.exp2(s - peak).astype(bf16), values)
        elif not exact:
            peak = before[1, at, :]
            shift = jnp.concatenate([peak] * (keys.shape[0] // 128), axis=1)
            state = dot(jnp.exp2(s - shift).astype(bf16), values) + before[0, at, :]
        else:
            old_peak = before[1, at, :]
            peak = jnp.max(s, axis=-1, keepdims=True)
            wide = jnp.maximum(peak, old_peak)
            peak = wide[:, :1]
            state = dot(jnp.exp2(s - peak).astype(bf16), values)
            state = state + before[0, at, :] * jnp.exp2(old_peak - wide)
        finish(k, at, state, peak)
        return state

    if loop:
        lax.fori_loop(0, steps, lambda k, carry: (step(k), carry)[1], 0)
        return None
    for k in range(steps):
        state = step(k)
        worst = state if worst is None else jnp.maximum(worst, state)
    return worst


def attend_more(queries, key_refs, rows, before, finish):
    worst = attend_part(queries, key_refs, rows, before, finish, exact=False)
    largest = jnp.max(jnp.where(low_lanes(TILE), worst, 0.0))

    @pl.when(jnp.logical_not(largest < 2.0**90))
    def _():
        attend_part(queries, key_refs, rows, before, finish, loop=True)


def keep_state(state_ref):
    def keep(k, at, state, peak):
        state_ref[0, at, :] = state
        state_ref[1, at, :] = jnp.broadcast_to(peak, state.shape)

    return keep


def attend_first_kernel(own_ref, q1_ref, q2_ref, q3_ref, queries_ref, state_ref):
    rows = q1_ref.shape[1] * 2
    unpack_queries((own_ref, q1_ref, q2_ref, q3_ref), (rows, 0, 0, 0), rows, queries_ref)
    attend_part(queries_ref, (own_ref,), rows, None, keep_state(state_ref))


def attend_next_kernel(queries_ref, kv1_ref, kv2_ref, before_ref, state_ref):
    rows = kv1_ref.shape[1]
    attend_more(queries_ref, (kv1_ref, kv2_ref), rows, before_ref, keep_state(state_ref))


def attend_last_kernel(place_ref, queries_ref, kv1_ref, kv2_ref, before_ref, out_ref):
    rows = kv1_ref.shape[1]
    unit = rows // 4
    half = unit // 2
    me = place_ref[0]
    low = low_lanes(half)
    lane = lax.broadcasted_iota(jnp.int32, (8, 128), 1)
    term = lax.rem(lane, 3)

    def send(k, at, state, peak):
        turned = swap(state)
        for t in range(TILE // rows):
            for u in range(4):
                at = (t * 4 + u) * unit
                top = slice(at, at + half)
                end = slice(at + half, at + unit)
                packed = jnp.where(low, turned[top], state[end]) / jnp.where(
                    low, state[top], turned[end]
                )
                sums = jnp.ones((8, 128), f32)
                peaks = jnp.zeros((8, 128), f32)
                for a in range(unit // 8):
                    here = jnp.logical_and(lane >= 3 * a, lane < 3 * a + 3)
                    part = slice(at + 8 * a, at + 8 * a + 8)
                    sums = jnp.where(here, state[part], sums)
                    peaks = jnp.where(here, peak[part], peaks)
                size = peaks + jnp.log2(sums)
                first = size.astype(bf16).astype(f32)
                second = (size - first).astype(bf16).astype(f32)
                stats = jnp.where(
                    term == 0, first, jnp.where(term == 1, second, size - first - second)
                )
                source = k * (TILE // rows) + t
                out_ref[source % 4, me ^ (source // 4), u * 32 : (u + 1) * 32] = jnp.concatenate(
                    [packed, stats], axis=0
                ).astype(bf16)

    attend_part(queries_ref, (kv1_ref, kv2_ref), rows, before_ref, send)


def write_query_kernel(mid_ref, gain_ref, w_ref, out_ref):
    out_ref[...] = dot(norm(mid_ref[...].astype(f32), gain_ref[...]), w_ref[...]).astype(bf16)


def back_kernel(
    place_ref, got_ref, latmid_ref, gwlat_ref, mid_ref, query_ref, wo0, wo1, wo2, wo3, wkv_hbm,
    tok_ref, lat_ref,
    wo, wkv, shares, sems,
):
    moves = [(source, wo.at[i]) for i, source in enumerate((wo0, wo1, wo2, wo3))]
    copies = [
        pltpu.make_async_copy(source, target, sems.at[i])
        for i, (source, target) in enumerate(moves + [(wkv_hbm, wkv)])
    ]
    for copy in copies:
        copy.start()
    me = place_ref[0]
    rows = latmid_ref.shape[0]
    half = rows // 2
    low = low_lanes(half)
    low8 = low_lanes(8)
    stats = got_ref[:, half:].astype(f32).reshape(64 * 8, 128)
    sizes = stats + pltpu.roll(stats, 127, 1) + pltpu.roll(stats, 126, 1)
    sizes = sizes.reshape(4, 4, 4, 8, 128)
    weights = jnp.exp2(sizes - jnp.max(sizes, axis=1, keepdims=True))
    weights = weights / jnp.sum(weights, axis=1, keepdims=True)
    shares[...] = weights.reshape(64, 8, 128)
    latents = latmid_ref[...].astype(f32)
    for d in range(4):
        heads = []
        for t in range(4):
            mixed = jnp.zeros((half, 128), f32)
            for x in range(4):
                source = t * 16 + x * 4 + (me ^ d)
                share = shares[source]
                spread = [
                    jnp.where(low8, share[:, 3 * b : 3 * b + 1], share[:, c : c + 1])
                    for b, c in ((b, 3 * (b + half // 8)) for b in range(half // 8))
                ]
                part = got_ref[source].astype(f32)[:half]
                mixed = mixed + part * jnp.concatenate(spread, axis=0)
            heads.append(mixed)
        pairs = []
        for one, two in ((heads[0], heads[1]), (heads[2], heads[3])):
            top = jnp.where(low, one, swap(two))
            end = jnp.where(low, swap(one), two)
            pairs.append(jnp.concatenate([top, end], axis=0).astype(bf16))
        copies[d].wait()
        latents = latents + dot(jnp.concatenate(pairs, axis=1), wo[d])
    latents = latents.astype(bf16)
    lat_ref[...] = latents
    normed = norm(latents.astype(f32), gwlat_ref[...])
    copies[4].wait()
    kv = dot(normed, wkv[...]).astype(bf16)
    head_of_row = lax.broadcasted_iota(jnp.int32, (8 * NLAT, 512), 0) // NLAT
    head_of_lane = lax.broadcasted_iota(jnp.int32, (8 * NLAT, 512), 1) // HEAD
    here = head_of_row == head_of_lane
    ones = jnp.where(here, 1.0, 0.0).astype(bf16)
    groups = rows // NLAT
    zero = jnp.zeros((8 * NLAT, 512), bf16)
    scores, values = [], []
    for g in range(groups):
        k = kv[g * NLAT : (g + 1) * NLAT, :512]
        v = kv[g * NLAT : (g + 1) * NLAT, 512:]
        k8 = jnp.where(here, jnp.concatenate([k] * 8, axis=0), zero)
        v8 = jnp.where(here, jnp.concatenate([v] * 8, axis=0), zero)
        values.append(jnp.concatenate([v8, ones], axis=1))
        scores.append(dot_t(k8, query_ref[g * G : (g + 1) * G, :]))
    s = (jnp.concatenate(scores, axis=1) * SCALE).reshape(8, NLAT, groups * G)
    w = jnp.exp2(s - jnp.max(s, axis=1, keepdims=True)).reshape(8 * NLAT, groups * G)
    turned = w.astype(bf16).T
    for g in range(groups):
        at = slice(g * G, (g + 1) * G)
        written = dot(turned[at], values[g])
        tok_ref[at, :] = (
            mid_ref[at, :].astype(f32) + written[:, :512] / written[:, 512:]
        ).astype(bf16)


def params(megabytes):
    return pltpu.CompilerParams(vmem_limit_bytes=megabytes * 1024 * 1024)


def cost(flops, bytes_accessed, transcendentals=0):
    return pl.CostEstimate(
        flops=int(flops), bytes_accessed=int(bytes_accessed), transcendentals=int(transcendentals)
    )


def local(
    tokens,
    latents,
    gain_self,
    w_qkv_tok,
    w_o_tok,
    gain_read,
    w_kv_read,
    gain_lat,
    w_q_read,
    gain_glob,
    w_qkv_glob,
    w_o_glob,
    gain_write,
    w_q_write,
    gain_wlat,
    w_kv_write,
):
    token_rows, width = tokens.shape
    lat_rows, lat_width = latents.shape
    row = lambda gain: gain.reshape(1, -1)
    other = [(0, 1), (1, 0)]
    w_o_core = lax.ppermute(w_o_glob, "core", other)
    w_o_yh = lax.ppermute(w_o_glob, "yh", other)
    vmem = pl.BlockSpec(memory_space=pltpu.VMEM)
    hbm = pl.BlockSpec(memory_space=pl.ANY)
    weights = (w_qkv_tok, w_o_tok, w_kv_read, w_q_read)
    tokens_mid, latents_mid, normed = pl.pallas_call(
        front_kernel,
        in_specs=[vmem] * 6 + [hbm] * 4,
        out_specs=[vmem] * 3,
        out_shape=[
            jax.ShapeDtypeStruct(tokens.shape, bf16),
            jax.ShapeDtypeStruct(latents.shape, bf16),
            jax.ShapeDtypeStruct(latents.shape, bf16),
        ],
        scratch_shapes=[pltpu.VMEM(w.shape, bf16) for w in weights]
        + [
            pltpu.VMEM((token_rows, w_qkv_tok.shape[1]), bf16),
            pltpu.VMEM((token_rows, w_kv_read.shape[1]), bf16),
            pltpu.VMEM((token_rows, width), bf16),
            pltpu.SemaphoreType.DMA((4,)),
        ],
        compiler_params=params(60),
        name="front",
    )(
        tokens, latents, row(gain_self), row(gain_read), row(gain_lat), row(gain_glob), *weights
    )

    block = lax.all_gather(normed, LAT, axis=0, tiled=True)
    block_rows = block.shape[0]
    half = block_rows // 2
    sent = pl.pallas_call(
        project_kernel,
        in_specs=[vmem] * 2,
        out_specs=vmem,
        out_shape=jax.ShapeDtypeStruct((4, block_rows + half, 128), bf16),
        compiler_params=params(32),
        name="project",
    )(block, w_qkv_glob)
    own = lax.all_to_all(sent, HEADS4, 0, 0, tiled=True)
    own_kv = own[:, :block_rows]
    own_q = own[:, block_rows:]
    others_q = [lax.ppermute(own_q, "x", [(i, i ^ k) for i in range(4)]) for k in (1, 2, 3)]
    ahead = [(i, (i + 1) % 4) for i in range(4)]
    behind = [(i, (i - 1) % 4) for i in range(4)]
    kv_ahead = lax.ppermute(own_kv, KEYS4, ahead)
    kv_behind = lax.ppermute(own_kv, KEYS4, behind)
    kv_far1 = lax.ppermute(kv_ahead[:2], KEYS4, ahead)
    kv_far2 = lax.ppermute(kv_behind[2:], KEYS4, behind)
    place = lax.axis_index("x").astype(jnp.int32).reshape(1)
    many = 16 * block_rows

    def part_cost(parts):
        return cost(parts * many * many * 64, many * 128 * 10, parts * many * many // 4)

    queries, state = pl.pallas_call(
        attend_first_kernel,
        in_specs=[vmem] * 4,
        out_specs=[vmem] * 2,
        out_shape=[
            jax.ShapeDtypeStruct((many, 128), bf16),
            jax.ShapeDtypeStruct((2, many, 128), f32),
        ],
        compiler_params=params(32),
        cost_estimate=part_cost(1),
        name="attend_first",
    )(own, *others_q)
    state = pl.pallas_call(
        attend_next_kernel,
        in_specs=[vmem] * 4,
        out_specs=vmem,
        out_shape=jax.ShapeDtypeStruct((2, many, 128), f32),
        compiler_params=params(32),
        cost_estimate=part_cost(2),
        name="attend_next",
    )(queries, kv_ahead, kv_behind, state)
    message = 2 * lat_rows // 3
    partial = pl.pallas_call(
        attend_last_kernel,
        in_specs=[pl.BlockSpec(memory_space=pltpu.SMEM)] + [vmem] * 4,
        out_specs=vmem,
        out_shape=jax.ShapeDtypeStruct((4, 4, 4 * message, 128), bf16),
        compiler_params=params(32),
        cost_estimate=part_cost(1),
        name="attend_last",
    )(place, queries, kv_far1, kv_far2, state)
    got = lax.all_to_all(partial.reshape(64, message, 128), OUT64, 0, 0, tiled=True)
    tokens_late, w_o_late, partial = lax.optimization_barrier((tokens_mid, w_o_yh, partial))
    w_o_both = lax.ppermute(w_o_late, "core", other)
    query = pl.pallas_call(
        write_query_kernel,
        in_specs=[vmem] * 3,
        out_specs=vmem,
        out_shape=jax.ShapeDtypeStruct(tokens.shape, bf16),
        compiler_params=params(32),
        cost_estimate=cost(2 * token_rows * width * width, token_rows * width * 4),
        name="write_query",
    )(tokens_late, row(gain_write), w_q_write)
    tokens_out, latents_out = pl.pallas_call(
        back_kernel,
        in_specs=[pl.BlockSpec(memory_space=pltpu.SMEM)] + [vmem] * 5 + [hbm] * 5,
        out_specs=[vmem] * 2,
        out_shape=[
            jax.ShapeDtypeStruct(tokens.shape, bf16),
            jax.ShapeDtypeStruct(latents.shape, bf16),
        ],
        scratch_shapes=[
            pltpu.VMEM((4,) + w_o_glob.shape, bf16),
            pltpu.VMEM(w_kv_write.shape, bf16),
            pltpu.VMEM((64, 8, 128), f32),
            pltpu.SemaphoreType.DMA((5,)),
        ],
        compiler_params=params(49),
        name="back",
    )(
        lax.axis_index(LAT).astype(jnp.int32).reshape(1),
        got,
        latents_mid,
        row(gain_wlat),
        tokens_late,
        query,
        w_o_glob,
        w_o_core,
        w_o_late,
        w_o_both,
        w_kv_write,
    )
    return (tokens_out, latents_out)


def solution(mesh):
    fine = Mesh(np.asarray(mesh.devices).reshape(SIZES), AXES)
    rows = P(AXES, None)
    placed = (
        rows,
        rows,
        P(),
        P(),
        P(),
        P(),
        P(),
        P(),
        P(),
        P(),
        P(None, None, LAT),
        P(LAT, None),
        P(),
        P(),
        P(),
        P(),
    )
    return jax.shard_map(
        local,
        mesh=fine,
        in_specs=placed,
        out_specs=(rows, rows),
        check_vma=False,
    )
```
